128 devices in a mesh: row: 8 (over y, core), col: 16 (over z, x).
Axes of the slice: x: 4, y: 4, z: 4, core: 2. Of those that a mesh axis runs over, the one named last changes fastest.
Arguments:
- attention_out: bfloat16 [16384, 8192], P('col', 'row'), may hold values from -6 to 6
- residual: bfloat16 [16384, 8192], P('col', 'row'), may hold values from -20 to 20
- trainer_shard: bfloat16 [8192, 8192], P(('row', 'col')), may hold values from -0.0625 to 0.0625
- norm_gain: bfloat16 [8192], P('row'), may hold values from 0.099609375 to 1.8984375
Outputs:
- served: bfloat16 [8192, 8192], P('row', 'col')
- hidden: bfloat16 [16384, 8192], P('col', 'row')
- normed: bfloat16 [16384, 8192], P('col', 'row')
The draws below stay inside these ranges and needn't reach their ends.
All inputs are finite; a program needn't handle non-finite values.
Results may differ from the reference program's by a relative error of at most 0.0049.
Values may be sent and summed in bfloat16 or wider, within the bound.
A program may use at most 128 MiB of HBM per device.

```python
import math
import jax
import jax.numpy as jnp
from jax import lax

D = 8192
TOKENS = 16384


def draw_residual(key, part):
    key = jax.random.fold_in(key, 7)
    key_rows, key_cols, key_base = jax.random.split(key, 3)
    ramp = jnp.exp(math.log(math.sqrt(3.0)) * jnp.arange(D, dtype=jnp.float32)[None, :] / D)
    rough = jnp.exp(jax.random.uniform(key_cols, (1, D), jnp.float32, math.log(0.4), math.log(2.5)))
    row_scale = jnp.exp(jax.random.uniform(key_rows, (TOKENS, 1), jnp.float32, math.log(0.3), math.log(3.0)))
    base = jnp.clip(jax.random.normal(key_base, (TOKENS, D), jnp.float32), -3.0, 3.0)
    values = 0.5 * base * row_scale * rough * ramp
    return values.astype(jnp.bfloat16)


def levels(rng, extent, cuts, low, high):
    def one(dim, shards_of):
        draws = jax.random.uniform(jax.random.fold_in(jax.random.fold_in(rng, 6), dim), (shards_of,), jnp.float32, low / len(cuts), high / len(cuts))
        return jnp.repeat(jnp.exp(draws), extent[dim] // shards_of).reshape((-1,) + (1,) * (len(extent) - dim - 1))

    level = one(*cuts[0])
    for cut in cuts[1:]:
        level = level * one(*cut)
    return level


def centred(rng, shape, deviation, most, pieces=(), kind=jnp.bfloat16):
    array = deviation * jax.random.normal(rng, shape, jnp.float32)
    if pieces:
        array = array * levels(rng, shape, pieces, -0.22, 0.18)
    return jnp.clip(array, -most, most).astype(kind)


def setup_inputs(seed: int = 0) -> dict:
    splits = jax.random.split(jax.random.key(seed), 5)
    attention_out = centred(splits[0], (TOKENS, D), 1.0, 6.0, ((0, 16), (1, 8)))
    residual = draw_residual(jax.random.fold_in(splits[4], 71), 0)
    trainer_shard = centred(splits[2], (D, D), D ** -0.5, 0.0625, ((0, 128),))
    norm_gain = jnp.clip(1.0 + 0.18 * jax.random.normal(splits[3], (D,), jnp.float32), 0.099609375, 1.8984375).astype(jnp.bfloat16)
    return {"attention_out": attention_out, "residual": residual, "trainer_shard": trainer_shard, "norm_gain": norm_gain}


def reference(attention_out, residual, trainer_shard, norm_gain):
    served = trainer_shard
    projected = lax.dot_general(attention_out, trainer_shard, (((1,), (1,)), ((), ())), preferred_element_type=jnp.float32)
    hidden = (residual.astype(jnp.float32) + projected).astype(jnp.bfloat16)
    hidden_wide = hidden.astype(jnp.float32)
    mean_square = lax.optimization_barrier(jnp.mean(hidden_wide * hidden_wide, axis=1, keepdims=True))
    normed = (hidden_wide * lax.rsqrt(mean_square + 1e-05) * norm_gain.astype(jnp.float32)[None, :]).astype(jnp.bfloat16)
    return (served, hidden, normed)
```

```python
import functools

import jax
import jax.numpy as jnp
from jax import lax
from jax.experimental import pallas as pl
from jax.experimental.pallas import tpu as pltpu
from jax.sharding import PartitionSpec as P

MESH = pl.DeviceIdType.MESH
NX = 4
NR = 8
F32 = jnp.float32
BF16 = jnp.bfloat16


def kernel(
    att, res, wsh, gain,
    served_o, hidden_o, normed_o,
    wbuf, abuf, acc, resv, hidv, normv, gainv, sums,
    w_send, w_recv, a_send, a_recv, b_send, b_recv, q_send, q_recv, l_sem,
):
    rows, kw = wsh.shape[0], abuf.shape[2]
    tokens = abuf.shape[1]
    half, quarter = rows // 2, rows // 4
    r, c = lax.axis_index("row"), lax.axis_index("col")
    my, core = r // 2, lax.rem(r, 2)
    mz, mx = c // NX, lax.rem(c, NX)

    def up(v):
        return lax.rem(v + 1, NX)

    def down(v):
        return lax.rem(v + NX - 1, NX)

    dev = [
        (r, mz * NX + up(mx)), (r, mz * NX + down(mx)),
        (r, up(mz) * NX + mx), (r, down(mz) * NX + mx),
    ]
    ydev = [(up(my) * 2 + core, c), (down(my) * 2 + core, c)]
    sibling = (my * 2 + 1 - core, c)
    peers = [(lax.rem(r + i, NR), c) for i in range(1, NR)]

    barrier = pltpu.get_barrier_semaphore()
    for d in dev + peers:
        pl.semaphore_signal(barrier, inc=1, device_id=d, device_id_type=MESH)

    def block(s):
        y = [my, up(my), down(my), lax.rem(my + 2, NX)][s // 2]
        return y * 2 + (core if s % 2 == 0 else 1 - core)

    kbs = [block(s) for s in range(NR)]

    def cols(kb):
        return pl.ds(pl.multiple_of(kb * kw, kw), kw)

    loads = {}
    def load(name, src, dst, i):
        loads[name] = pltpu.make_async_copy(src, dst, l_sem.at[i])
        loads[name].start()

    for s in range(NR):
        load("w%d" % s, wsh.at[:, cols(kbs[s])], wbuf.at[kbs[s], mz, mx], s)
    load("a", att, abuf.at[r], 8)
    load("res", res, resv, 9)
    load("gain", gain, gainv, 10)
    pl.semaphore_wait(barrier, len(dev) + len(peers))

    sent = []

    def copy(src, dst, ss, rs, d):
        return pltpu.make_async_remote_copy(
            src_ref=src, dst_ref=dst, send_sem=ss, recv_sem=rs, device_id=d, device_id_type=MESH
        )

    def go(src, dst, ss, rs, d):
        cp = copy(src, dst, ss, rs, d)
        cp.start()
        sent.append(cp)

    def w_ref(kb, h, stage, direction, sender):
        axis_x = direction < 2
        plus = direction % 2 == 0
        pos = mx if axis_x else mz
        pos = {0: pos, 1: up(pos), -1: down(pos)}[sender]
        if stage in (1, 3):
            pos = down(pos) if plus else up(pos)
        if stage < 2:
            if stage == 0:
                rs = pl.ds(h * half, half)
            else:
                rs = pl.ds(h * half + (0 if plus else quarter), quarter)
            z, x = (mz, pos) if axis_x else (pos, mx)
            return wbuf.at[kb, z, x, rs, :]
        if stage == 2:
            others = pl.ds(0, NX)
        else:
            others = pl.ds(0 if plus else NX // 2, NX // 2)
        rs = pl.ds(h * half, half)
        if axis_x:
            return wbuf.at[kb, others, pos, rs, :]
        return wbuf.at[kb, pos, others, rs, :]

    def w_dirs(stage):
        first = stage < 2
        return [(0 if (d < 2) == first else 1, d) for d in range(4)]

    def w_start(stage, s):
        for h, d in w_dirs(stage):
            ref = w_ref(kbs[s], h, stage, d, 0)
            src = ref
            if stage == 0:
                src = wsh.at[pl.ds(h * half, half), cols(kbs[s])]
            go(src, ref, w_send.at[stage, d, s], w_recv.at[stage, d, s], dev[d])

    def w_wait(stage, s):
        for h, d in w_dirs(stage):
            ref = w_ref(kbs[s], h, stage, d, -1 if d % 2 == 0 else 1)
            copy(ref, ref, w_send.at[stage, d, s], w_recv.at[stage, d, s], dev[d]).wait_recv()

    qt = tokens // 4

    def a_ref(y, q, k):
        return abuf.at[y * 2 + k, pl.ds(q * qt, qt), :]

    def a_start(hop):
        for q in range(4):
            for d in range(2):
                if hop == 0:
                    go(att.at[pl.ds(q * qt, qt), :], a_ref(my, q, core), a_send.at[0, d, q], a_recv.at[0, d, q], ydev[d])
                elif q // 2 == d:
                    ref = a_ref(down(my) if d == 0 else up(my), q, core)
                    go(ref, ref, a_send.at[1, d, q], a_recv.at[1, d, q], ydev[d])

    def a_wait(hop):
        for q in range(4):
            for d in range(2):
                if hop == 0:
                    ref = a_ref(down(my) if d == 0 else up(my), q, core)
                elif q // 2 == d:
                    ref = a_ref(lax.rem(my + 2, NX), q, core)
                else:
                    continue
                copy(ref, ref, a_send.at[hop, d, q], a_recv.at[hop, d, q], ydev[d]).wait_recv()

    def b_y(i):
        return [my, up(my), down(my), lax.rem(my + 2, NX)][i]

    def b_start(i):
        src = att if i == 0 else abuf.at[b_y(i) * 2 + core]
        go(src, abuf.at[b_y(i) * 2 + core], b_send.at[i], b_recv.at[i], sibling)

    def b_wait(i):
        ref = abuf.at[b_y(i) * 2 + 1 - core]
        copy(ref, ref, b_send.at[i], b_recv.at[i], sibling).wait_recv()

    nt = NX * rows
    def compute(s):
        kb = kbs[s]

        @pl.loop(0, NX)
        def _(z):
            w = wbuf[kb, z].reshape(nt, kw)
            at = pl.ds(pl.multiple_of(z * nt, nt), nt)
            p = lax.dot_general(abuf[kb], w, (((1,), (1,)), ((), ())), preferred_element_type=F32)
            if s == 0:
                acc[:, at] = p
            else:
                acc[:, at] += p

    a_start(0)
    for s in range(NR):
        w_start(0, s)
    b_start(0)
    for s in range(NR):
        w_wait(0, s)
        w_start(1, s)
    for s in range(NR + 2):
        if s < NR:
            w_wait(1, s)
            loads["w%d" % s].wait()
            w_start(2, s)
        if 1 <= s <= NR:
            w_wait(2, s - 1)
            w_start(3, s - 1)
        if s == 4:
            a_wait(0)
            a_start(1)
            b_start(1)
            b_start(2)
        if s == 7:
            a_wait(1)
            b_start(3)
        if s >= 2:
            w_wait(3, s - 2)
            if s == 2:
                loads["a"].wait()
            elif s == 3:
                b_wait(0)
            elif s == 5:
                b_wait(1)
            elif s == 7:
                b_wait(2)
            elif s == 9:
                b_wait(3)
            compute(s - 2)

    kb_s, part = c // 2, lax.rem(c, 2)
    served = pltpu.make_async_copy(
        wbuf.at[kb_s, :, :, :, pl.ds(pl.multiple_of(part * (kw // 2), kw // 2), kw // 2)], served_o, l_sem.at[11])
    served.start()

    loads["res"].wait()
    loads["gain"].wait()
    nb = tokens // 128
    lanes = kw // 128

    @pl.loop(0, nb)
    def _(t):
        at = pl.ds(pl.multiple_of(t * 128, 128), 128)
        h = (resv[at, :].astype(F32) + acc[at, :]).astype(BF16)
        hidv[at, :] = h
        hw = h.astype(F32)
        sq = hw * hw
        p = sq[:, 0:128]
        for i in range(1, lanes):
            p = p + sq[:, i * 128:(i + 1) * 128]
        sums[r, pl.ds(t, 1), :] = jnp.sum(p.T, axis=0, keepdims=True)

    for i, d in enumerate(peers):
        go(sums.at[r], sums.at[r], q_send.at[i], q_recv.at[i], d)
    hidden = pltpu.make_async_copy(hidv, hidden_o, l_sem.at[12])
    hidden.start()
    for i in range(1, NR):
        ref = sums.at[lax.rem(r + NR - i, NR)]
        copy(ref, ref, q_send.at[i - 1], q_recv.at[i - 1], peers[i - 1]).wait_recv()
    total = sums[0]
    for i in range(1, NR):
        total = total + sums[i]
    inv = lax.rsqrt(total / (NR * kw) + 1e-05)
    g = gainv[...].astype(F32)
    for t in range(nb):
        scale = jnp.broadcast_to(inv[t:t + 1, :], (128, 128)).T
        for i in range(lanes):
            ls = slice(i * 128, (i + 1) * 128)
            ts = slice(t * 128, (t + 1) * 128)
            normv[ts, ls] = (hidv[ts, ls].astype(F32) * scale * g[:, ls]).astype(BF16)
    normed = pltpu.make_async_copy(normv, normed_o, l_sem.at[13])
    normed.start()
    served.wait()
    hidden.wait()
    normed.wait()
    for cp in sent:
        cp.wait_send()


def per_device(attention_out, residual, trainer_shard, norm_gain):
    tokens, kw = attention_out.shape
    rows, width = trainer_shard.shape
    anywhere = pl.BlockSpec(memory_space=pl.ANY)
    dma = pltpu.SemaphoreType.DMA
    served, hidden, normed = pl.pallas_call(
        kernel,
        out_shape=(
            jax.ShapeDtypeStruct((NX, NX, rows, kw // 2), BF16),
            jax.ShapeDtypeStruct((tokens, kw), BF16),
            jax.ShapeDtypeStruct((tokens, kw), BF16),
        ),
        in_specs=[anywhere] * 4,
        out_specs=(anywhere,) * 3,
        scratch_shapes=[
            pltpu.VMEM((NR, NX, NX, rows, kw), BF16),
            pltpu.VMEM((NR, tokens, kw), BF16),
            pltpu.VMEM((tokens, kw), F32),
            pltpu.VMEM((tokens, kw), BF16),
            pltpu.VMEM((tokens, kw), BF16),
            pltpu.VMEM((tokens, kw), BF16),
            pltpu.VMEM((1, kw), BF16),
            pltpu.VMEM((NR, tokens // 128, 128), F32),
            dma((4, 4, NR)), dma((4, 4, NR)),
            dma((2, 2, 4)), dma((2, 2, 4)),
            dma((4,)), dma((4,)),
            dma((NR - 1,)), dma((NR - 1,)),
            dma((14,)),
        ],
        compiler_params=pltpu.CompilerParams(
            collective_id=0, has_side_effects=True, vmem_limit_bytes=56 * 1024 * 1024
        ),
        cost_estimate=pl.CostEstimate(
            flops=2 * tokens * kw * width, bytes_accessed=10 * tokens * kw, transcendentals=tokens
        ),
    )(attention_out, residual, trainer_shard, norm_gain.reshape(1, kw))
    return (served.reshape(NX * NX * rows, kw // 2), hidden, normed)


def solution(mesh):
    in_specs = (P("col", "row"), P("col", "row"), P(("row", "col"), None), P("row"))
    out_specs = (P("row", "col"), P("col", "row"), P("col", "row"))
    return jax.shard_map(
        per_device, mesh=mesh, in_specs=in_specs, out_specs=out_specs, check_vma=False
    )
```

```python
import functools

import jax
import jax.numpy as jnp
from jax import lax
from jax.experimental import pallas as pl
from jax.experimental.pallas import tpu as pltpu
from jax.sharding import PartitionSpec as P

MESH = pl.DeviceIdType.MESH
NX = 4
NR = 8
F32 = jnp.float32
BF16 = jnp.bfloat16


def kernel(
    att, res, wsh,
    served_o, hidden_o, total_o,
    wbuf, abuf, acc, resv, squares, sums,
    w_send, w_recv, a_send, a_recv, b_send, b_recv, q_send, q_recv, l_sem,
):
    rows, kw = wsh.shape[0], abuf.shape[2]
    tokens = abuf.shape[1]
    half, quarter = rows // 2, rows // 4
    r, c = lax.axis_index("row"), lax.axis_index("col")
    my, core = r // 2, lax.rem(r, 2)
    mz, mx = c // NX, lax.rem(c, NX)

    def up(v):
        return lax.rem(v + 1, NX)

    def down(v):
        return lax.rem(v + NX - 1, NX)

    dev = [
        (r, mz * NX + up(mx)), (r, mz * NX + down(mx)),
        (r, up(mz) * NX + mx), (r, down(mz) * NX + mx),
    ]
    ydev = [(up(my) * 2 + core, c), (down(my) * 2 + core, c)]
    sibling = (my * 2 + 1 - core, c)
    peers = [(lax.rem(r + i, NR), c) for i in range(1, NR)]

    barrier = pltpu.get_barrier_semaphore()
    for d in dev + peers:
        pl.semaphore_signal(barrier, inc=1, device_id=d, device_id_type=MESH)

    def block(s):
        y = [my, up(my), down(my), lax.rem(my + 2, NX)][s // 2]
        return y * 2 + (core if s % 2 == 0 else 1 - core)

    kbs = [block(s) for s in range(NR)]

    def cols(kb):
        return pl.ds(pl.multiple_of(kb * kw, kw), kw)

    loads = {}
    def load(name, src, dst, i):
        loads[name] = pltpu.make_async_copy(src, dst, l_sem.at[i])
        loads[name].start()

    for s in range(NR):
        load("w%d" % s, wsh.at[:, cols(kbs[s])], wbuf.at[kbs[s], mz, mx], s)
    load("a", att, abuf.at[r], 8)
    load("res", res, resv, 9)
    pl.semaphore_wait(barrier, len(dev) + len(peers))

    sent = []

    def copy(src, dst, ss, rs, d):
        return pltpu.make_async_remote_copy(
            src_ref=src, dst_ref=dst, send_sem=ss, recv_sem=rs, device_id=d, device_id_type=MESH
        )

    def go(src, dst, ss, rs, d):
        cp = copy(src, dst, ss, rs, d)
        cp.start()
        sent.append(cp)

    def w_ref(kb, h, stage, direction, sender):
        axis_x = direction < 2
        plus = direction % 2 == 0
        pos = mx if axis_x else mz
        pos = {0: pos, 1: up(pos), -1: down(pos)}[sender]
        if stage in (1, 3):
            pos = down(pos) if plus else up(pos)
        if stage < 2:
            if stage == 0:
                rs = pl.ds(h * half, half)
            else:
                rs = pl.ds(h * half + (0 if plus else quarter), quarter)
            z, x = (mz, pos) if axis_x else (pos, mx)
            return wbuf.at[kb, z, x, rs, :]
        if stage == 2:
            others = pl.ds(0, NX)
        else:
            others = pl.ds(0 if plus else NX // 2, NX // 2)
        rs = pl.ds(h * half, half)
        if axis_x:
            return wbuf.at[kb, others, pos, rs, :]
        return wbuf.at[kb, pos, others, rs, :]

    def w_dirs(stage):
        first = stage < 2
        return [(0 if (d < 2) == first else 1, d) for d in range(4)]

    def w_start(stage, s):
        for h, d in w_dirs(stage):
            ref = w_ref(kbs[s], h, stage, d, 0)
            src = ref
            if stage == 0:
                src = wsh.at[pl.ds(h * half, half), cols(kbs[s])]
            go(src, ref, w_send.at[stage, d, s], w_recv.at[stage, d, s], dev[d])

    def w_wait(stage, s):
        for h, d in w_dirs(stage):
            ref = w_ref(kbs[s], h, stage, d, -1 if d % 2 == 0 else 1)
            copy(ref, ref, w_send.at[stage, d, s], w_recv.at[stage, d, s], dev[d]).wait_recv()

    qt = tokens // 4

    def a_ref(y, q, k):
        return abuf.at[y * 2 + k, pl.ds(q * qt, qt), :]

    def a_start(hop):
        for q in range(4):
            for d in range(2):
                if hop == 0:
                    go(att.at[pl.ds(q * qt, qt), :], a_ref(my, q, core), a_send.at[0, d, q], a_recv.at[0, d, q], ydev[d])
                elif q // 2 == d:
                    ref = a_ref(down(my) if d == 0 else up(my), q, core)
                    go(ref, ref, a_send.at[1, d, q], a_recv.at[1, d, q], ydev[d])

    def a_wait(hop):
        for q in range(4):
            for d in range(2):
                if hop == 0:
                    ref = a_ref(down(my) if d == 0 else up(my), q, core)
                elif q // 2 == d:
                    ref = a_ref(lax.rem(my + 2, NX), q, core)
                else:
                    continue
                copy(ref, ref, a_send.at[hop, d, q], a_recv.at[hop, d, q], ydev[d]).wait_recv()

    def b_y(i):
        return [my, up(my), down(my), lax.rem(my + 2, NX)][i]

    def b_start(i):
        src = att if i == 0 else abuf.at[b_y(i) * 2 + core]
        go(src, abuf.at[b_y(i) * 2 + core], b_send.at[i], b_recv.at[i], sibling)

    def b_wait(i):
        ref = abuf.at[b_y(i) * 2 + 1 - core]
        copy(ref, ref, b_send.at[i], b_recv.at[i], sibling).wait_recv()

    nt = NX * rows
    def compute(s):
        kb = kbs[s]

        @pl.loop(0, NX)
        def _(z):
            w = wbuf[kb, z].reshape(nt, kw)
            at = pl.ds(pl.multiple_of(z * nt, nt), nt)
            p = lax.dot_general(abuf[kb], w, (((1,), (1,)), ((), ())), preferred_element_type=F32)
            if s == 0:
                acc[:, at] = p
            elif s < NR - 1:
                acc[:, at] += p
            else:
                h = (resv[:, at].astype(F32) + (acc[:, at] + p)).astype(BF16)
                hidden_o[:, at] = h
                hw = h.astype(F32)
                sq = hw * hw
                part = sq[:, 0:128]
                for i in range(1, nt // 128):
                    part = part + sq[:, i * 128:(i + 1) * 128]
                squares[...] += part

    squares[...] = jnp.zeros_like(squares)
    a_start(0)
    for s in range(NR):
        w_start(0, s)
    b_start(0)
    for s in range(NR):
        w_wait(0, s)
        w_start(1, s)
    for s in range(NR + 2):
        if s < NR:
            w_wait(1, s)
            loads["w%d" % s].wait()
            w_start(2, s)
        if 1 <= s <= NR:
            w_wait(2, s - 1)
            w_start(3, s - 1)
        if s == 4:
            a_wait(0)
            a_start(1)
            b_start(1)
            b_start(2)
        if s == 7:
            a_wait(1)
            b_start(3)
        if s >= 2:
            w_wait(3, s - 2)
            if s == 2:
                loads["a"].wait()
            elif s == 3:
                b_wait(0)
            elif s == 5:
                b_wait(1)
            elif s == 7:
                b_wait(2)
            elif s == 9:
                b_wait(3)
            if s == NR + 1:
                loads["res"].wait()
            compute(s - 2)

    kb_s, part = c // 2, lax.rem(c, 2)
    served = pltpu.make_async_copy(
        wbuf.at[kb_s, :, :, :, pl.ds(pl.multiple_of(part * (kw // 2), kw // 2), kw // 2)], served_o, l_sem.at[11])
    served.start()

    for t in range(tokens // 128):
        sums[r, t:t + 1, :] = jnp.sum(squares[t * 128:(t + 1) * 128, :].T, axis=0, keepdims=True)
    for i, d in enumerate(peers):
        go(sums.at[r], sums.at[r], q_send.at[i], q_recv.at[i], d)
    for i in range(1, NR):
        ref = sums.at[lax.rem(r + NR - i, NR)]
        copy(ref, ref, q_send.at[i - 1], q_recv.at[i - 1], peers[i - 1]).wait_recv()
    total = sums[0]
    for i in range(1, NR):
        total = total + sums[i]
    total_o[...] = total
    served.wait()
    for cp in sent:
        cp.wait_send()


def finish(served, hidden, total, gain, served_o, hidden_o, normed_o, normv, sem):
    tokens, kw = hidden.shape
    copies = [
        pltpu.make_async_copy(hidden, hidden_o, sem.at[0]),
        pltpu.make_async_copy(served, served_o, sem.at[1]),
    ]
    for cp in copies:
        cp.start()
    inv = lax.rsqrt(total[...] / (NR * kw) + 1e-05)
    g = gain[...].astype(F32)[None, :]
    for t in range(tokens // 128):
        ts = slice(t * 128, (t + 1) * 128)
        scale = jnp.broadcast_to(inv[t:t + 1, :], (128, 128)).T
        for i in range(kw // 128):
            ls = slice(i * 128, (i + 1) * 128)
            normv[ts, ls] = (hidden[ts, ls].astype(F32) * scale * g[:, ls]).astype(BF16)
        cp = pltpu.make_async_copy(normv.at[ts, :], normed_o.at[ts, :], sem.at[2 + t])
        cp.start()
        copies.append(cp)
    for cp in copies:
        cp.wait()


def per_device(attention_out, residual, trainer_shard, norm_gain):
    tokens, kw = attention_out.shape
    rows, width = trainer_shard.shape
    hbm = pl.BlockSpec(memory_space=pltpu.HBM)
    vmem = pl.BlockSpec(memory_space=pltpu.VMEM)
    dma = pltpu.SemaphoreType.DMA
    shapes = (
        jax.ShapeDtypeStruct((NX, NX, rows, kw // 2), BF16),
        jax.ShapeDtypeStruct((tokens, kw), BF16),
        jax.ShapeDtypeStruct((tokens, kw), BF16),
    )
    served, hidden, total = pl.pallas_call(
        kernel,
        out_shape=tuple(pltpu.VMEM(a.shape, a.dtype) for a in shapes[:2]) + (pltpu.VMEM((tokens // 128, 128), F32),),
        in_specs=[hbm] * 3,
        out_specs=(vmem,) * 3,
        scratch_shapes=[
            pltpu.VMEM((NR, NX, NX, rows, kw), BF16),
            pltpu.VMEM((NR, tokens, kw), BF16),
            pltpu.VMEM((tokens, kw), F32),
            pltpu.VMEM((tokens, kw), BF16),
            pltpu.VMEM((tokens, 128), F32),
            pltpu.VMEM((NR, tokens // 128, 128), F32),
            dma((4, 4, NR)), dma((4, 4, NR)),
            dma((2, 2, 4)), dma((2, 2, 4)),
            dma((4,)), dma((4,)),
            dma((NR - 1,)), dma((NR - 1,)),
            dma((12,)),
        ],
        compiler_params=pltpu.CompilerParams(
            collective_id=0, has_side_effects=True, vmem_limit_bytes=50 * 1024 * 1024
        ),
        cost_estimate=pl.CostEstimate(
            flops=2 * tokens * kw * width, bytes_accessed=10 * tokens * kw, transcendentals=0
        ),
    )(attention_out, residual, trainer_shard)
    served, hidden, normed = pl.pallas_call(
        finish,
        out_shape=shapes,
        in_specs=[vmem] * 4,
        out_specs=(hbm,) * 3,
        scratch_shapes=[pltpu.VMEM((tokens, kw), BF16), dma((2 + tokens // 128,))],
        compiler_params=pltpu.CompilerParams(vmem_limit_bytes=16 * 1024 * 1024),
        cost_estimate=pl.CostEstimate(
            flops=4 * tokens * kw, bytes_accessed=5 * tokens * kw, transcendentals=tokens
        ),
    )(served, hidden, total, norm_gain)
    return (served.reshape(NX * NX * rows, kw // 2), hidden, normed)


def solution(mesh):
    in_specs = (P("col", "row"), P("col", "row"), P(("row", "col"), None), P("row"))
    out_specs = (P("row", "col"), P("col", "row"), P("col", "row"))
    return jax.shard_map(
        per_device, mesh=mesh, in_specs=in_specs, out_specs=out_specs, check_vma=False
    )
```

```python
import functools

import jax
import jax.numpy as jnp
from jax import lax
from jax.experimental import pallas as pl
from jax.experimental.pallas import tpu as pltpu
from jax.sharding import PartitionSpec as P

MESH = pl.DeviceIdType.MESH
NX = 4
NR = 8
F32 = jnp.float32
BF16 = jnp.bfloat16


def level(v):
    return lax.rem(v + v // 2, 2)


def pair(v):
    return v + 1 - 2 * lax.rem(v, 2)


def mate(v):
    return NX - 1 - v


def kernel(
    att, res, wsh,
    served_o, hidden_o, total_o,
    wbuf, wother, abuf, acc, obuf, ibuf, resv, squares, sums,
    c_send, c_recv, p_send, p_recv, n_send, n_recv, y_send, y_recv, s_send, s_recv, o_send, o_recv, q_send, q_recv, l_sem,
):
    rows, kh = wsh.shape[0], abuf.shape[3]
    kw, tokens = 2 * kh, abuf.shape[2]
    part, qt = rows // 2, tokens // 4
    ht = tokens // 2
    r, c = lax.axis_index("row"), lax.axis_index("col")
    y, core = r // 2, lax.rem(r, 2)
    z, x = c // NX, lax.rem(c, NX)
    px, pz, mx, mz = pair(x), pair(z), mate(x), mate(z)
    colour = lax.rem(level(x) + level(z), 2)
    up, down, across = lax.rem(y + 1, NX), lax.rem(y + NX - 1, NX), lax.rem(y + 2, NX)

    px_dev, pz_dev, diag_dev = (r, z * NX + px), (r, pz * NX + x), (r, pz * NX + px)
    mates = [(r, z * NX + mx), (r, mz * NX + x)]
    ydev = [(up * 2 + core, c), (down * 2 + core, c)]
    sibling = (y * 2 + 1 - core, c)
    peers = [(lax.rem(r + i, NR), c) for i in range(1, NR)]

    barrier = pltpu.get_barrier_semaphore()
    greeted = [px_dev, pz_dev, diag_dev] + mates + peers
    for d in greeted:
        pl.semaphore_signal(barrier, inc=1, device_id=d, device_id_type=MESH)

    def cols(k, col):
        b = lax.rem(col + lax.rem(k, 2) + level(k // 2), 2)
        return pl.ds(pl.multiple_of(k * kw + b * kh, kh), kh)

    def my_cols(col):
        b = lax.rem(col + core + level(y), 2)
        return pl.ds(pl.multiple_of(b * kh, kh), kh)

    loads = {}

    def load(name, src, dst):
        loads[name] = pltpu.make_async_copy(src, dst, l_sem.at[len(loads)])
        loads[name].start()

    for p in range(2):
        for k in range(NR):
            ps, ks = pl.ds(p * part, part), pl.ds(k * kh, kh)
            load(("w", p, k), wsh.at[ps, cols(k, colour)], wbuf.at[z, x, ps, ks])
    for p in range(2):
        for k in range(NR):
            ps, ks = pl.ds(p * part, part), pl.ds(k * kh, kh)
            load(("v", p, k), wsh.at[ps, cols(k, 1 - colour)], wother.at[ps, ks])
    load("a", att.at[:, my_cols(colour)], abuf.at[0, r])
    load("res", res, resv)
    pl.semaphore_wait(barrier, len(greeted))

    sent = []

    def copy(src, dst, ss, rs, d):
        return pltpu.make_async_remote_copy(
            src_ref=src, dst_ref=dst, send_sem=ss, recv_sem=rs, device_id=d, device_id_type=MESH
        )

    def go(src, dst, ss, rs, d):
        cp = copy(src, dst, ss, rs, d)
        cp.start()
        sent.append(cp)

    def arrived(ref, ss, rs, d):
        copy(ref, ref, ss, rs, d).wait_recv()

    def source(at_z, at_x, s):
        return (pair(at_z) if s >= 2 else at_z), (pair(at_x) if s % 2 else at_x)

    def w_ref(at_z, at_x, s, p):
        sz, sx = source(at_z, at_x, s)
        return wbuf.at[sz, sx, pl.ds(p * part, part), :]

    def pair_start(s, p):
        ps = pl.ds(p * part, part)
        src = wbuf.at[z, x, ps, :] if s == 3 else wother.at[ps, :]
        d = [px_dev, pz_dev, diag_dev][s - 1]
        go(src, wbuf.at[z, x, ps, :], p_send.at[s - 1, p], p_recv.at[s - 1, p], d)

    def pair_wait(s, p):
        d = [px_dev, pz_dev, diag_dev][s - 1]
        arrived(w_ref(z, x, s, p), p_send.at[s - 1, p], p_recv.at[s - 1, p], d)

    def mate_start(s, p):
        i = 2 * s + p
        for l in range(2):
            ref = w_ref(z, x, s, p)
            go(ref, ref, c_send.at[l, i], c_recv.at[l, i], mates[l])

    def mate_wait(l, s, p):
        i = 2 * s + p
        ref = w_ref(z, mx, s, p) if l == 0 else w_ref(mz, x, s, p)
        arrived(ref, c_send.at[l, i], c_recv.at[l, i], mates[l])

    def forward_start(s):
        ref = w_ref(z, mx, s, 0)
        go(ref, ref, c_send.at[1, 8 + s], c_recv.at[1, 8 + s], mates[1])
        ref = w_ref(mz, x, s, 1)
        go(ref, ref, c_send.at[0, 8 + s], c_recv.at[0, 8 + s], mates[0])

    def forward_wait(s):
        for l in range(2):
            arrived(w_ref(mz, mx, s, 1 - l), c_send.at[l, 8 + s], c_recv.at[l, 8 + s], mates[l])

    chunks = [(0, 0), (1, 0), (1, ht), (0, ht)]

    def a_ref(i, at_y, k, lo, n):
        o, t0 = chunks[i]
        return abuf.at[o, at_y * 2 + k, pl.ds(t0 + lo, n), :]

    def nbr_start(i):
        o, t0 = chunks[i]
        d = pz_dev if i == 1 else px_dev
        go(att.at[pl.ds(t0, ht), my_cols(1 - colour)], a_ref(i, y, core, 0, ht), n_send.at[i - 1], n_recv.at[i - 1], d)

    def nbr_wait(i):
        d = pz_dev if i == 1 else px_dev
        arrived(a_ref(i, y, core, 0, ht), n_send.at[i - 1], n_recv.at[i - 1], d)

    def y_start(i):
        for piece in range(2):
            for d in range(2):
                lo = (piece if d == 0 else 1 - piece) * qt
                ref = a_ref(i, y, core, lo, qt)
                go(ref, ref, y_send.at[i, piece, d], y_recv.at[i, piece, d], ydev[d])

    def y_wait(i, piece):
        for d in range(2):
            lo = (piece if d == 0 else 1 - piece) * qt
            ref = a_ref(i, down if d == 0 else up, core, lo, qt)
            arrived(ref, y_send.at[i, piece, d], y_recv.at[i, piece, d], ydev[d])

    def y_forward(i):
        for d in range(2):
            ref = a_ref(i, down if d == 0 else up, core, d * qt, qt)
            go(ref, ref, y_send.at[i, 2, d], y_recv.at[i, 2, d], ydev[d])

    def y_last(i):
        for d in range(2):
            ref = a_ref(i, across, core, d * qt, qt)
            arrived(ref, y_send.at[i, 2, d], y_recv.at[i, 2, d], ydev[d])

    ys = [y, up, down, across]

    def sib_start(i, j):
        ref = a_ref(i, ys[j], core, 0, ht)
        go(ref, ref, s_send.at[i, j], s_recv.at[i, j], sibling)

    def sib_wait(i):
        for j in range(4):
            arrived(a_ref(i, ys[j], 1 - core, 0, ht), s_send.at[i, j], s_recv.at[i, j], sibling)

    nb = 2 * rows

    def blocks(i):
        qz = z + (i // 2) * (mz - z)
        qx = x + lax.rem(i, 2) * (mx - x)
        return [qz * 2 + qx // 2, pair(qz) * 2 + qx // 2]

    def product(o, t0, ns):
        w = []
        for n in ns:
            w.append(wbuf[n // 2, pl.ds(2 * lax.rem(n, 2), 2)].reshape(nb, NR * kh))
        w = w[0] if len(w) == 1 else jnp.concatenate(w, axis=0)
        a = jnp.concatenate([abuf[o, k, pl.ds(t0, ht), :] for k in range(NR)], axis=1)
        return lax.dot_general(a, w, (((1,), (1,)), ((), ())), preferred_element_type=F32)

    def out_ref(buf, h, n):
        return buf.at[n, pl.ds(h * ht, ht), :]

    def nbr_product(h, ns):
        v = product(1, h * ht, ns).astype(BF16)
        for j, n in enumerate(ns):
            obuf[n, pl.ds(h * ht, ht), :] = v[:, j * nb:(j + 1) * nb]
        for n in ns:
            copy(out_ref(obuf, h, n), out_ref(ibuf, h, n), o_send.at[h, n], o_recv.at[h, n],
                 pz_dev if h == 0 else px_dev).start()

    def own_product(h, i):
        ns = blocks(i)
        v = product(0, h * ht, ns)
        for j, n in enumerate(ns):
            ts = pl.ds(h * ht, ht)
            at = pl.ds(pl.multiple_of(n * nb, nb), nb)
            acc[n, ts, :] = v[:, j * nb:(j + 1) * nb] + resv[ts, at].astype(F32)

    for p in range(2):
        for k in range(NR):
            loads["w", p, k].wait()
        mate_start(0, p)
        if p == 0:
            nbr_start(1)
            loads["a"].wait()
            y_start(0)
    for p in range(2):
        for k in range(NR):
            loads["v", p, k].wait()
        pair_start(1, p)
        pair_start(2, p)
    sib_start(0, 0)
    pair_wait(1, 0)
    mate_start(1, 0)
    nbr_start(2)
    y_wait(0, 0)
    y_forward(0)
    pair_wait(1, 1)
    mate_start(1, 1)
    pair_start(3, 0)
    pair_start(3, 1)
    nbr_wait(1)
    y_start(1)
    sib_start(1, 0)
    y_wait(0, 1)
    sib_start(0, 1)
    sib_start(0, 2)
    pair_wait(2, 0)
    mate_start(2, 0)
    y_last(0)
    sib_start(0, 3)
    pair_wait(2, 1)
    mate_start(2, 1)
    y_wait(1, 0)
    y_forward(1)
    nbr_wait(2)
    y_start(2)
    sib_start(2, 0)
    pair_wait(3, 0)
    mate_start(3, 0)
    y_wait(1, 1)
    sib_start(1, 1)
    sib_start(1, 2)
    pair_wait(3, 1)
    mate_start(3, 1)
    y_last(1)
    sib_start(1, 3)
    for l in range(2):
        for p in range(2):
            mate_wait(l, 0, p)
    forward_start(0)
    sib_wait(0)
    loads["res"].wait()
    own_product(0, 0)
    sib_wait(1)
    nbr_product(0, blocks(0))
    y_wait(2, 0)
    y_forward(2)
    y_start(3)
    sib_start(3, 0)
    for s in (1, 2):
        for l in range(2):
            for p in range(2):
                mate_wait(l, s, p)
        forward_start(s)
    y_wait(2, 1)
    sib_start(2, 1)
    sib_start(2, 2)
    for l in range(2):
        for p in range(2):
            mate_wait(l, 3, p)
    forward_start(3)

    @pl.loop(1, 3)
    def _(i):
        nbr_product(0, blocks(i))

    y_last(2)
    sib_start(2, 3)
    forward_wait(0)
    sib_wait(2)

    @pl.loop(0, 3)
    def _(i):
        nbr_product(1, blocks(i))

    y_wait(3, 0)
    y_forward(3)
    forward_wait(1)

    @pl.loop(0, 2)
    def _(h):
        ns = blocks(3)[:1]
        v = product(1, pl.multiple_of(h * ht, ht), ns).astype(BF16)
        obuf[ns[0], pl.ds(pl.multiple_of(h * ht, ht), ht), :] = v

    n = blocks(3)[0]
    for h in range(2):
        copy(out_ref(obuf, h, n), out_ref(ibuf, h, n), o_send.at[h, n], o_recv.at[h, n], pz_dev if h == 0 else px_dev).start()

    @pl.loop(1, 3)
    def _(i):
        own_product(0, i)

    y_wait(3, 1)
    sib_start(3, 1)
    sib_start(3, 2)
    forward_wait(2)
    forward_wait(3)

    @pl.loop(0, 2)
    def _(h):
        ns = blocks(3)[1:]
        v = product(1, pl.multiple_of(h * ht, ht), ns).astype(BF16)
        obuf[ns[0], pl.ds(pl.multiple_of(h * ht, ht), ht), :] = v

    n = blocks(3)[1]
    for h in range(2):
        copy(out_ref(obuf, h, n), out_ref(ibuf, h, n), o_send.at[h, n], o_recv.at[h, n], pz_dev if h == 0 else px_dev).start()
    y_last(3)
    sib_start(3, 3)
    own_product(0, 3)
    sib_wait(3)

    @pl.loop(0, 4)
    def _(i):
        own_product(1, i)

    served = pltpu.make_async_copy(
        wbuf.at[:, :, :, pl.ds(pl.multiple_of((c // 2) * kh, kh), kh)], served_o, l_sem.at[len(loads)])
    served.start()

    squares[...] = jnp.zeros_like(squares)
    for n in range(NR):
        for h in range(2):
            arrived(out_ref(ibuf, h, n), o_send.at[h, n], o_recv.at[h, n], pz_dev if h == 0 else px_dev)

    for n in range(NR):
        h = (acc[n] + ibuf[n].astype(F32)).astype(BF16)
        hidden_o[:, n * nb:(n + 1) * nb] = h
        hw = h.astype(F32)
        squares[...] += hw * hw

    for t in range(tokens // 128):
        sums[r, t:t + 1, :] = jnp.sum(squares[t * 128:(t + 1) * 128, :].T, axis=0, keepdims=True)
    for i, d in enumerate(peers):
        go(sums.at[r], sums.at[r], q_send.at[i], q_recv.at[i], d)
    for i in range(1, NR):
        arrived(sums.at[lax.rem(r + NR - i, NR)], q_send.at[i - 1], q_recv.at[i - 1], peers[i - 1])
    total = sums[0]
    for i in range(1, NR):
        total = total + sums[i]
    total_o[...] = total
    served.wait()
    for n in range(NR):
        for h in range(2):
            copy(out_ref(obuf, h, n), out_ref(ibuf, h, n), o_send.at[h, n], o_recv.at[h, n],
                 pz_dev if h == 0 else px_dev).wait_send()
    for cp in sent:
        cp.wait_send()


def finish(served, hidden, total, gain, served_o, hidden_o, normed_o, normv, sem):
    tokens, kw = hidden.shape
    copies = [
        pltpu.make_async_copy(hidden, hidden_o, sem.at[0]),
        pltpu.make_async_copy(served, served_o, sem.at[1]),
    ]
    for cp in copies:
        cp.start()
    inv = lax.rsqrt(total[...] / (NR * kw) + 1e-05)
    g = gain[...].astype(F32)[None, :]
    for t in range(tokens // 128):
        ts = slice(t * 128, (t + 1) * 128)
        scale = jnp.broadcast_to(inv[t:t + 1, :], (128, 128)).T
        for i in range(kw // 128):
            ls = slice(i * 128, (i + 1) * 128)
            normv[ts, ls] = (hidden[ts, ls].astype(F32) * scale * g[:, ls]).astype(BF16)
        cp = pltpu.make_async_copy(normv.at[ts, :], normed_o.at[ts, :], sem.at[2 + t])
        cp.start()
        copies.append(cp)
    for cp in copies:
        cp.wait()


def per_device(attention_out, residual, trainer_shard, norm_gain):
    tokens, kw = attention_out.shape
    rows, width = trainer_shard.shape
    kh = kw // 2
    hbm = pl.BlockSpec(memory_space=pltpu.HBM)
    vmem = pl.BlockSpec(memory_space=pltpu.VMEM)
    dma = pltpu.SemaphoreType.DMA
    shapes = (
        jax.ShapeDtypeStruct((NX, NX, rows, kw // 2), BF16),
        jax.ShapeDtypeStruct((tokens, kw), BF16),
        jax.ShapeDtypeStruct((tokens, kw), BF16),
    )
    served, hidden, total = pl.pallas_call(
        kernel,
        out_shape=tuple(pltpu.VMEM(a.shape, a.dtype) for a in shapes[:2]) + (pltpu.VMEM((tokens // 128, 128), F32),),
        in_specs=[hbm] * 3,
        out_specs=(vmem,) * 3,
        scratch_shapes=[
            pltpu.VMEM((NX, NX, rows, NR * kh), BF16),
            pltpu.VMEM((rows, NR * kh), BF16),
            pltpu.VMEM((2, NR, tokens, kh), BF16),
            pltpu.VMEM((NR, tokens, 2 * rows), F32),
            pltpu.VMEM((NR, tokens, 2 * rows), BF16),
            pltpu.VMEM((NR, tokens, 2 * rows), BF16),
            pltpu.VMEM((tokens, kw), BF16),
            pltpu.VMEM((tokens, 128), F32),
            pltpu.VMEM((NR, tokens // 128, 128), F32),
            dma((2, 12)), dma((2, 12)),
            dma((3, 2)), dma((3, 2)),
            dma((2,)), dma((2,)),
            dma((4, 3, 2)), dma((4, 3, 2)),
            dma((4, 4)), dma((4, 4)),
            dma((2, NR)), dma((2, NR)),
            dma((NR - 1,)), dma((NR - 1,)),
            dma((4 * NR + 3,)),
        ],
        compiler_params=pltpu.CompilerParams(
            collective_id=0, has_side_effects=True, vmem_limit_bytes=50 * 1024 * 1024
        ),
        cost_estimate=pl.CostEstimate(
            flops=2 * tokens * kw * width, bytes_accessed=10 * tokens * kw, transcendentals=0
        ),
    )(attention_out, residual, trainer_shard)
    served, hidden, normed = pl.pallas_call(
        finish,
        out_shape=shapes,
        in_specs=[vmem] * 4,
        out_specs=(hbm,) * 3,
        scratch_shapes=[pltpu.VMEM((tokens, kw), BF16), dma((2 + tokens // 128,))],
        compiler_params=pltpu.CompilerParams(vmem_limit_bytes=16 * 1024 * 1024),
        cost_estimate=pl.CostEstimate(
            flops=4 * tokens * kw, bytes_accessed=5 * tokens * kw, transcendentals=tokens
        ),
    )(served, hidden, total, norm_gain)
    return (served.reshape(NX * NX * rows, kw // 2), hidden, normed)


def solution(mesh):
    in_specs = (P("col", "row"), P("col", "row"), P(("row", "col"), None), P("row"))
    out_specs = (P("row", "col"), P("col", "row"), P("col", "row"))
    return jax.shard_map(
        per_device, mesh=mesh, in_specs=in_specs, out_specs=out_specs, check_vma=False
    )
```

```python
import functools

import jax
import jax.numpy as jnp
from jax import lax
from jax.experimental import pallas as pl
from jax.experimental.pallas import tpu as pltpu
from jax.sharding import PartitionSpec as P

MESH = pl.DeviceIdType.MESH
NX = 4
NR = 8
F32 = jnp.float32
BF16 = jnp.bfloat16


def level(v):
    return lax.rem(v + v // 2, 2)


def pair(v):
    return v + 1 - 2 * lax.rem(v, 2)


def mate(v):
    return NX - 1 - v


def kernel(
    att, res, wsh,
    served_o, hidden_o, total_o,
    wbuf, wother, abuf, acc, obuf, ibuf, resv, early, squares, sums,
    c_send, c_recv, p_send, p_recv, n_send, n_recv, y_send, y_recv, s_send, s_recv, o_send, o_recv, q_send, q_recv, l_sem,
):
    rows, kh = wsh.shape[0], abuf.shape[3]
    kw, tokens = 2 * kh, abuf.shape[2]
    part, ht = rows // 2, tokens // 2
    width = NR * kh
    late = 3 * width // 4
    r, c = lax.axis_index("row"), lax.axis_index("col")
    y, core = r // 2, lax.rem(r, 2)
    z, x = c // NX, lax.rem(c, NX)
    px, pz, mx, mz = pair(x), pair(z), mate(x), mate(z)
    colour = lax.rem(level(x) + level(z), 2)
    up, down, across = lax.rem(y + 1, NX), lax.rem(y + NX - 1, NX), lax.rem(y + 2, NX)

    px_dev, pz_dev, diag_dev = (r, z * NX + px), (r, pz * NX + x), (r, pz * NX + px)
    mates = [(r, z * NX + mx), (r, mz * NX + x)]
    ydev = [(up * 2 + core, c), (down * 2 + core, c)]
    sibling = (y * 2 + 1 - core, c)
    peers = [(lax.rem(r + i, NR), c) for i in range(1, NR)]

    barrier = pltpu.get_barrier_semaphore()
    greeted = [px_dev, pz_dev, diag_dev] + mates + peers
    for d in greeted:
        pl.semaphore_signal(barrier, inc=1, device_id=d, device_id_type=MESH)

    def cols(k, col):
        b = lax.rem(col + lax.rem(k, 2) + level(k // 2), 2)
        return pl.ds(pl.multiple_of(k * kw + b * kh, kh), kh)

    def my_cols(col):
        b = lax.rem(col + core + level(y), 2)
        return pl.ds(pl.multiple_of(b * kh, kh), kh)

    loads = {}

    def load(name, src, dst):
        loads[name] = pltpu.make_async_copy(src, dst, l_sem.at[len(loads)])
        loads[name].start()

    for p in range(2):
        for k in range(NR):
            ps, ks = pl.ds(p * part, part), pl.ds(k * kh, kh)
            load(("w", p, k), wsh.at[ps, cols(k, colour)], wbuf.at[z, x, ps, ks])
    for p in range(2):
        for k in range(NR):
            ps, ks = pl.ds(p * part, part), pl.ds(k * kh, kh)
            load(("v", p, k), wsh.at[ps, cols(k, 1 - colour)], wother.at[ps, ks])
    load("a", att.at[:, my_cols(colour)], abuf.at[0, r])
    load("res", res, resv)
    pl.semaphore_wait(barrier, len(greeted))

    sent = []

    def copy(src, dst, ss, rs, d):
        return pltpu.make_async_remote_copy(
            src_ref=src, dst_ref=dst, send_sem=ss, recv_sem=rs, device_id=d, device_id_type=MESH
        )

    def go(src, dst, ss, rs, d):
        cp = copy(src, dst, ss, rs, d)
        cp.start()
        sent.append(cp)

    def arrived(ref, ss, rs, d):
        copy(ref, ref, ss, rs, d).wait_recv()

    def source(at_z, at_x, s):
        return (pair(at_z) if s >= 2 else at_z), (pair(at_x) if s % 2 else at_x)

    def w_ref(at_z, at_x, s, p, lo=0, hi=width):
        sz, sx = source(at_z, at_x, s)
        return wbuf.at[sz, sx, pl.ds(p * part, part), pl.ds(lo, hi - lo)]

    def pair_start(s, p):
        ps = pl.ds(p * part, part)
        src = wbuf.at[z, x, ps, :] if s == 3 else wother.at[ps, :]
        d = [px_dev, pz_dev, diag_dev][s - 1]
        go(src, wbuf.at[z, x, ps, :], p_send.at[s - 1, p], p_recv.at[s - 1, p], d)

    def pair_wait(s, p):
        d = [px_dev, pz_dev, diag_dev][s - 1]
        arrived(w_ref(z, x, s, p), p_send.at[s - 1, p], p_recv.at[s - 1, p], d)

    def mate_start(s, p):
        i = 2 * s + p
        for l in range(2):
            ref = w_ref(z, x, s, p)
            go(ref, ref, c_send.at[l, i], c_recv.at[l, i], mates[l])

    def mate_wait(l, s, p):
        i = 2 * s + p
        ref = w_ref(z, mx, s, p) if l == 0 else w_ref(mz, x, s, p)
        arrived(ref, c_send.at[l, i], c_recv.at[l, i], mates[l])

    pieces = [(0, 0, width), (1, 0, width), (2, 0, late), (3, 0, late), (2, late, width), (3, late, width)]

    def forward_start(j):
        s, lo, hi = pieces[j]
        ref = w_ref(z, mx, s, 0, lo, hi)
        go(ref, ref, c_send.at[1, 8 + j], c_recv.at[1, 8 + j], mates[1])
        ref = w_ref(mz, x, s, 1, lo, hi)
        go(ref, ref, c_send.at[0, 8 + j], c_recv.at[0, 8 + j], mates[0])

    def forward_wait(j):
        s, lo, hi = pieces[j]
        for l in range(2):
            arrived(w_ref(mz, mx, s, 1 - l, lo, hi), c_send.at[l, 8 + j], c_recv.at[l, 8 + j], mates[l])

    t1, t2 = 3 * tokens // 8, 6 * tokens // 8
    chunks = [(0, 0, t1), (1, 0, ht), (1, ht, ht), (0, t1, t2 - t1), (0, t2, tokens - t2)]

    def a_ref(i, at_y, k, lo, n):
        o, t0, _ = chunks[i]
        return abuf.at[o, at_y * 2 + k, pl.ds(t0 + lo, n), :]

    def nbr_start(i):
        t0 = chunks[i][1]
        d = pz_dev if i == 1 else px_dev
        go(att.at[pl.ds(t0, ht), my_cols(1 - colour)], a_ref(i, y, core, 0, ht), n_send.at[i - 1], n_recv.at[i - 1], d)

    def nbr_wait(i):
        d = pz_dev if i == 1 else px_dev
        arrived(a_ref(i, y, core, 0, ht), n_send.at[i - 1], n_recv.at[i - 1], d)

    def y_start(i):
        n = chunks[i][2] // 2
        for piece in range(2):
            for d in range(2):
                ref = a_ref(i, y, core, (piece if d == 0 else 1 - piece) * n, n)
                go(ref, ref, y_send.at[i, piece, d], y_recv.at[i, piece, d], ydev[d])

    def y_wait(i, piece):
        n = chunks[i][2] // 2
        for d in range(2):
            ref = a_ref(i, down if d == 0 else up, core, (piece if d == 0 else 1 - piece) * n, n)
            arrived(ref, y_send.at[i, piece, d], y_recv.at[i, piece, d], ydev[d])

    def y_forward(i):
        n = chunks[i][2] // 2
        for d in range(2):
            ref = a_ref(i, down if d == 0 else up, core, d * n, n)
            go(ref, ref, y_send.at[i, 2, d], y_recv.at[i, 2, d], ydev[d])

    def y_last(i):
        n = chunks[i][2] // 2
        for d in range(2):
            ref = a_ref(i, across, core, d * n, n)
            arrived(ref, y_send.at[i, 2, d], y_recv.at[i, 2, d], ydev[d])

    ys = [y, up, down, across]

    def sib_start(i, j):
        ref = a_ref(i, ys[j], core, 0, chunks[i][2])
        go(ref, ref, s_send.at[i, j], s_recv.at[i, j], sibling)

    def sib_wait(i, js=(0, 1, 2, 3)):
        for j in js:
            arrived(a_ref(i, ys[j], 1 - core, 0, chunks[i][2]), s_send.at[i, j], s_recv.at[i, j], sibling)

    nb = 2 * rows

    def blocks(i):
        def pick(*of):
            return jnp.where(i == 0, of[0], jnp.where(i == 1, of[1], jnp.where(i == 2, of[2], of[3])))

        def block(along_z, along_x, second):
            bz, bx = z + along_z * (mz - z), x + along_x * (mx - x)
            return (bz + second * (pair(bz) - bz)) * 2 + bx // 2

        return [
            block(pick(0, 1, 0, 1), pick(0, 0, 1, 1), pick(0, 0, 1, 0)),
            block(pick(0, 0, 1, 1), pick(1, 0, 0, 1), pick(0, 1, 1, 1)),
        ]

    def dot(a, w):
        return lax.dot_general(a, w, (((1,), (1,)), ((), ())), preferred_element_type=F32)

    def product(o, t0, nt, ns, lo=0, hi=width):
        w = [wbuf[n // 2, pl.ds(2 * lax.rem(n, 2), 2), :, lo:hi].reshape(nb, hi - lo) for n in ns]
        a = [abuf[o, k, pl.ds(t0, nt), :] for k in range(lo // kh, hi // kh)]
        return dot(jnp.concatenate(a, axis=1), w[0] if len(w) == 1 else jnp.concatenate(w, axis=0))

    def out_copy(h, n):
        ts = pl.ds(h * ht, ht)
        return copy(obuf.at[n, ts, :], ibuf.at[n, ts, :], o_send.at[h, n], o_recv.at[h, n], pz_dev if h == 0 else px_dev)

    def nbr_product(h, ns):
        v = product(1, h * ht, ht, ns).astype(BF16)
        for j, n in enumerate(ns):
            obuf[n, pl.ds(h * ht, ht), :] = v[:, j * nb:(j + 1) * nb]
        for n in ns:
            out_copy(h, n).start()

    def own_product(ci, i):
        _, t0, nt = chunks[ci]
        ns = blocks(i)
        v = product(0, t0, nt, ns)
        for j, n in enumerate(ns):
            ts = pl.ds(t0, nt)
            at = pl.ds(pl.multiple_of(n * nb, nb), nb)
            acc[n, ts, :] = v[:, j * nb:(j + 1) * nb] + resv[ts, at].astype(F32)

    zero = r // NR

    def each(lo, hi, f):
        pl.loop(zero + lo, zero + hi)(f)

    for p in range(2):
        for k in range(NR):
            loads["w", p, k].wait()
        mate_start(0, p)
        if p == 0:
            nbr_start(1)
            loads["a"].wait()
            y_start(0)
    for p in range(2):
        for k in range(NR):
            loads["v", p, k].wait()
        pair_start(1, p)
        pair_start(2, p)
    sib_start(0, 0)
    y_wait(0, 0)
    y_forward(0)
    pair_wait(1, 0)
    mate_start(1, 0)
    nbr_start(2)
    y_wait(0, 1)
    sib_start(0, 1)
    sib_start(0, 2)
    pair_wait(1, 1)
    mate_start(1, 1)
    pair_start(3, 0)
    pair_start(3, 1)
    nbr_wait(1)
    y_start(1)
    sib_start(1, 0)
    y_last(0)
    sib_start(0, 3)
    pair_wait(2, 0)
    mate_start(2, 0)
    y_wait(1, 0)
    y_forward(1)
    pair_wait(2, 1)
    mate_start(2, 1)
    nbr_wait(2)
    y_start(2)
    sib_start(2, 0)
    y_wait(1, 1)
    sib_start(1, 1)
    sib_start(1, 2)
    sib_wait(0)
    loads["res"].wait()
    for s in range(2):
        for l in range(2):
            for p in range(2):
                mate_wait(l, s, p)
    each(0, 1, lambda i: own_product(0, i))
    pair_wait(3, 0)
    mate_start(3, 0)
    y_last(1)
    sib_start(1, 3)
    sib_wait(1)
    each(0, 1, lambda i: nbr_product(0, blocks(i)))
    pair_wait(3, 1)
    mate_start(3, 1)
    forward_start(0)
    forward_start(1)
    y_wait(2, 0)
    y_forward(2)
    y_start(3)
    sib_start(3, 0)
    each(1, 2, lambda i: nbr_product(0, blocks(i)))
    each(1, 2, lambda i: own_product(0, i))
    for l in range(2):
        for p in range(2):
            mate_wait(l, 2, p)
    forward_start(2)
    y_wait(2, 1)
    sib_start(2, 1)
    sib_start(2, 2)
    for l in range(2):
        for p in range(2):
            mate_wait(l, 3, p)
    for j in range(3, 6):
        forward_start(j)
    each(2, 3, lambda i: nbr_product(0, blocks(i)))
    y_last(2)
    sib_start(2, 3)
    sib_wait(2)
    each(0, 2, lambda i: nbr_product(1, blocks(i)))
    y_wait(3, 0)
    y_forward(3)
    y_start(4)
    sib_start(4, 0)
    each(2, 3, lambda i: nbr_product(1, blocks(i)))
    each(2, 3, lambda i: own_product(0, i))
    y_wait(3, 1)
    sib_start(3, 1)
    sib_start(3, 2)
    forward_wait(0)
    forward_wait(1)
    first, last = blocks(3)

    @pl.loop(0, 2)
    def _(h):
        ts = pl.ds(pl.multiple_of(h * ht, ht), ht)
        obuf[first, ts, :] = product(1, ts.start, ht, [first]).astype(BF16)

    for h in range(2):
        out_copy(h, first).start()
    y_last(3)
    sib_start(3, 3)
    sib_wait(3)
    each(0, 1, lambda i: own_product(3, i))
    y_wait(4, 0)
    y_forward(4)
    each(1, 3, lambda i: own_product(3, i))
    forward_wait(2)
    forward_wait(3)

    @pl.loop(0, 2)
    def _(h):
        ts = pl.ds(pl.multiple_of(h * ht, ht), ht)
        early[ts, :] = product(1, ts.start, ht, [last], 0, late)

    y_wait(4, 1)
    sib_start(4, 1)
    sib_start(4, 2)
    forward_wait(4)
    forward_wait(5)

    @pl.loop(0, 2)
    def _(h):
        ts = pl.ds(pl.multiple_of(h * ht, ht), ht)
        obuf[last, ts, :] = (early[ts, :] + product(1, ts.start, ht, [last], late, width)).astype(BF16)

    for h in range(2):
        out_copy(h, last).start()
    y_last(4)
    sib_start(4, 3)
    each(3, 4, lambda i: own_product(0, i))
    each(3, 4, lambda i: own_product(3, i))
    sib_wait(4)
    each(0, 4, lambda i: own_product(4, i))

    served = pltpu.make_async_copy(
        wbuf.at[:, :, :, pl.ds(pl.multiple_of((c // 2) * kh, kh), kh)], served_o, l_sem.at[len(loads)])
    served.start()

    squares[...] = jnp.zeros_like(squares)

    def finish_block(n):
        for h in range(2):
            out_copy(h, n).wait_recv()
        hid = (acc[n] + ibuf[n].astype(F32)).astype(BF16)
        hidden_o[:, pl.ds(pl.multiple_of(n * nb, nb), nb)] = hid
        wide = hid.astype(F32)
        squares[...] += wide * wide

    @pl.loop(1, NR)
    def _(i):
        finish_block(lax.rem(last + i, NR))

    finish_block(last)

    for t in range(tokens // 128):
        sums[r, t:t + 1, :] = jnp.sum(squares[t * 128:(t + 1) * 128, :].T, axis=0, keepdims=True)
    for i, d in enumerate(peers):
        go(sums.at[r], sums.at[r], q_send.at[i], q_recv.at[i], d)
    for i in range(1, NR):
        arrived(sums.at[lax.rem(r + NR - i, NR)], q_send.at[i - 1], q_recv.at[i - 1], peers[i - 1])
    total = sums[0]
    for i in range(1, NR):
        total = total + sums[i]
    total_o[...] = total
    served.wait()
    for n in range(NR):
        for h in range(2):
            out_copy(h, n).wait_send()
    for cp in sent:
        cp.wait_send()


def finish(served, hidden, total, gain, served_o, hidden_o, normed_o, normv, sem):
    tokens, kw = hidden.shape
    copies = [
        pltpu.make_async_copy(hidden, hidden_o, sem.at[0]),
        pltpu.make_async_copy(served, served_o, sem.at[1]),
    ]
    for cp in copies:
        cp.start()
    inv = lax.rsqrt(total[...] / (NR * kw) + 1e-05)
    g = gain[...].astype(F32)[None, :]
    for t in range(tokens // 128):
        ts = slice(t * 128, (t + 1) * 128)
        scale = jnp.broadcast_to(inv[t:t + 1, :], (128, 128)).T
        for i in range(kw // 128):
            ls = slice(i * 128, (i + 1) * 128)
            normv[ts, ls] = (hidden[ts, ls].astype(F32) * scale * g[:, ls]).astype(BF16)
        cp = pltpu.make_async_copy(normv.at[ts, :], normed_o.at[ts, :], sem.at[2 + t])
        cp.start()
        copies.append(cp)
    for cp in copies:
        cp.wait()


def per_device(attention_out, residual, trainer_shard, norm_gain):
    tokens, kw = attention_out.shape
    rows, width = trainer_shard.shape
    kh = kw // 2
    hbm = pl.BlockSpec(memory_space=pltpu.HBM)
    vmem = pl.BlockSpec(memory_space=pltpu.VMEM)
    dma = pltpu.SemaphoreType.DMA
    shapes = (
        jax.ShapeDtypeStruct((NX, NX, rows, kw // 2), BF16),
        jax.ShapeDtypeStruct((tokens, kw), BF16),
        jax.ShapeDtypeStruct((tokens, kw), BF16),
    )
    served, hidden, total = pl.pallas_call(
        kernel,
        out_shape=tuple(pltpu.VMEM(a.shape, a.dtype) for a in shapes[:2]) + (pltpu.VMEM((tokens // 128, 128), F32),),
        in_specs=[hbm] * 3,
        out_specs=(vmem,) * 3,
        scratch_shapes=[
            pltpu.VMEM((NX, NX, rows, NR * kh), BF16),
            pltpu.VMEM((rows, NR * kh), BF16),
            pltpu.VMEM((2, NR, tokens, kh), BF16),
            pltpu.VMEM((NR, tokens, 2 * rows), F32),
            pltpu.VMEM((NR, tokens, 2 * rows), BF16),
            pltpu.VMEM((NR, tokens, 2 * rows), BF16),
            pltpu.VMEM((tokens, kw), BF16),
            pltpu.VMEM((tokens, 2 * rows), F32),
            pltpu.VMEM((tokens, 128), F32),
            pltpu.VMEM((NR, tokens // 128, 128), F32),
            dma((2, 14)), dma((2, 14)),
            dma((3, 2)), dma((3, 2)),
            dma((2,)), dma((2,)),
            dma((5, 3, 2)), dma((5, 3, 2)),
            dma((5, 4)), dma((5, 4)),
            dma((2, NR)), dma((2, NR)),
            dma((NR - 1,)), dma((NR - 1,)),
            dma((4 * NR + 3,)),
        ],
        compiler_params=pltpu.CompilerParams(
            collective_id=0, has_side_effects=True, vmem_limit_bytes=50 * 1024 * 1024
        ),
        cost_estimate=pl.CostEstimate(
            flops=2 * tokens * kw * width, bytes_accessed=10 * tokens * kw, transcendentals=0
        ),
    )(attention_out, residual, trainer_shard)
    served, hidden, normed = pl.pallas_call(
        finish,
        out_shape=shapes,
        in_specs=[vmem] * 4,
        out_specs=(hbm,) * 3,
        scratch_shapes=[pltpu.VMEM((tokens, kw), BF16), dma((2 + tokens // 128,))],
        compiler_params=pltpu.CompilerParams(vmem_limit_bytes=16 * 1024 * 1024),
        cost_estimate=pl.CostEstimate(
            flops=4 * tokens * kw, bytes_accessed=5 * tokens * kw, transcendentals=tokens
        ),
    )(served, hidden, total, norm_gain)
    return (served.reshape(NX * NX * rows, kw // 2), hidden, normed)


def solution(mesh):
    in_specs = (P("col", "row"), P("col", "row"), P(("row", "col"), None), P("row"))
    out_specs = (P("row", "col"), P("col", "row"), P("col", "row"))
    return jax.shard_map(
        per_device, mesh=mesh, in_specs=in_specs, out_specs=out_specs, check_vma=False
    )
```

```python
import functools

import jax
import jax.numpy as jnp
from jax import lax
from jax.experimental import pallas as pl
from jax.experimental.pallas import tpu as pltpu
from jax.sharding import PartitionSpec as P

MESH = pl.DeviceIdType.MESH
NX = 4
NR = 8
F32 = jnp.float32
BF16 = jnp.bfloat16


def level(v):
    return lax.rem(v + v // 2, 2)


def pair(v):
    return v + 1 - 2 * lax.rem(v, 2)


def mate(v):
    return NX - 1 - v


def kernel(
    att, res, wsh,
    served_o, hidden_o, total_o,
    wbuf, wother, abuf, acc, obuf, ibuf, resv, early, squares, sums,
    c_send, c_recv, p_send, p_recv, n_send, n_recv, y_send, y_recv, s_send, s_recv, o_send, o_recv, q_send, q_recv, l_sem, gate,
):
    rows, kh = wsh.shape[0], abuf.shape[3]
    kw, tokens = 2 * kh, abuf.shape[2]
    part, ht = rows // 2, tokens // 2
    width = NR * kh
    late = 3 * width // 4
    r, c = lax.axis_index("row"), lax.axis_index("col")
    y, core = r // 2, lax.rem(r, 2)
    z, x = c // NX, lax.rem(c, NX)
    px, pz, mx, mz = pair(x), pair(z), mate(x), mate(z)
    colour = lax.rem(level(x) + level(z), 2)
    up, down, across = lax.rem(y + 1, NX), lax.rem(y + NX - 1, NX), lax.rem(y + 2, NX)

    px_dev, pz_dev, diag_dev = (r, z * NX + px), (r, pz * NX + x), (r, pz * NX + px)
    mates = [(r, z * NX + mx), (r, mz * NX + x)]
    ydev = [(up * 2 + core, c), (down * 2 + core, c)]
    sibling = (y * 2 + 1 - core, c)
    peers = [(lax.rem(r + i, NR), c) for i in range(1, NR)]

    barrier = pltpu.get_barrier_semaphore()
    greeted = [px_dev, pz_dev, diag_dev] + mates + peers
    for d in greeted:
        pl.semaphore_signal(barrier, inc=1, device_id=d, device_id_type=MESH)

    def cols(k, col):
        b = lax.rem(col + lax.rem(k, 2) + level(k // 2), 2)
        return pl.ds(pl.multiple_of(k * kw + b * kh, kh), kh)

    def my_cols(col):
        b = lax.rem(col + core + level(y), 2)
        return pl.ds(pl.multiple_of(b * kh, kh), kh)

    loads = {}

    def load(name, src, dst):
        loads[name] = pltpu.make_async_copy(src, dst, l_sem.at[len(loads)])
        loads[name].start()

    for p in range(2):
        for k in range(NR):
            ps, ks = pl.ds(p * part, part), pl.ds(k * kh, kh)
            load(("w", p, k), wsh.at[ps, cols(k, colour)], wbuf.at[z, x, ps, ks])
    for p in range(2):
        for k in range(NR):
            ps, ks = pl.ds(p * part, part), pl.ds(k * kh, kh)
            load(("v", p, k), wsh.at[ps, cols(k, 1 - colour)], wother.at[ps, ks])
    load("a", att.at[:, my_cols(colour)], abuf.at[0, r])
    load("res", res, resv)
    pl.semaphore_wait(barrier, len(greeted))

    sent = []

    def copy(src, dst, ss, rs, d):
        return pltpu.make_async_remote_copy(
            src_ref=src, dst_ref=dst, send_sem=ss, recv_sem=rs, device_id=d, device_id_type=MESH
        )

    def go(src, dst, ss, rs, d):
        cp = copy(src, dst, ss, rs, d)
        cp.start()
        sent.append(cp)

    def arrived(ref, ss, rs, d):
        copy(ref, ref, ss, rs, d).wait_recv()

    def source(at_z, at_x, s):
        return (pair(at_z) if s >= 2 else at_z), (pair(at_x) if s % 2 else at_x)

    def w_ref(at_z, at_x, s, p, lo=0, hi=width):
        sz, sx = source(at_z, at_x, s)
        return wbuf.at[sz, sx, pl.ds(p * part, part), pl.ds(lo, hi - lo)]

    def pair_start(s, p):
        ps = pl.ds(p * part, part)
        src = wbuf.at[z, x, ps, :] if s == 3 else wother.at[ps, :]
        d = [px_dev, pz_dev, diag_dev][s - 1]
        go(src, wbuf.at[z, x, ps, :], p_send.at[s - 1, p], p_recv.at[s - 1, p], d)

    def pair_wait(s, p):
        d = [px_dev, pz_dev, diag_dev][s - 1]
        arrived(w_ref(z, x, s, p), p_send.at[s - 1, p], p_recv.at[s - 1, p], d)

    def mate_start(s, p):
        i = 2 * s + p
        for l in range(2):
            ref = w_ref(z, x, s, p)
            go(ref, ref, c_send.at[l, i], c_recv.at[l, i], mates[l])

    def mate_wait(l, s, p):
        i = 2 * s + p
        ref = w_ref(z, mx, s, p) if l == 0 else w_ref(mz, x, s, p)
        arrived(ref, c_send.at[l, i], c_recv.at[l, i], mates[l])

    pieces = [(0, 0, width), (1, 0, width), (2, 0, late), (3, 0, late), (2, late, width), (3, late, width)]

    def forward_start(j):
        s, lo, hi = pieces[j]
        ref = w_ref(z, mx, s, 0, lo, hi)
        go(ref, ref, c_send.at[1, 8 + j], c_recv.at[1, 8 + j], mates[1])
        ref = w_ref(mz, x, s, 1, lo, hi)
        go(ref, ref, c_send.at[0, 8 + j], c_recv.at[0, 8 + j], mates[0])

    def forward_wait(j):
        s, lo, hi = pieces[j]
        for l in range(2):
            arrived(w_ref(mz, mx, s, 1 - l, lo, hi), c_send.at[l, 8 + j], c_recv.at[l, 8 + j], mates[l])

    t1, t2 = 3 * tokens // 8, 6 * tokens // 8
    groups = [(0, 8 * tokens // 16), (8 * tokens // 16, 8 * tokens // 16)]
    chunks = [(0, 0, t1), (1, *groups[0]), (1, *groups[1]), (0, t1, t2 - t1), (0, t2, tokens - t2)]

    def a_ref(i, at_y, k, lo, n):
        o, t0, _ = chunks[i]
        return abuf.at[o, at_y * 2 + k, pl.ds(t0 + lo, n), :]

    def nbr_ref(g):
        return abuf.at[1, r, pl.ds(*groups[g]), :]

    def nbr_start(g):
        src = att.at[pl.ds(*groups[g]), my_cols(1 - colour)]
        go(src, nbr_ref(g), n_send.at[g], n_recv.at[g], pz_dev if g == 0 else px_dev)

    def nbr_wait(g):
        arrived(nbr_ref(g), n_send.at[g], n_recv.at[g], pz_dev if g == 0 else px_dev)

    def y_start(i):
        n = chunks[i][2] // 2
        for piece in range(2):
            for d in range(2):
                ref = a_ref(i, y, core, (piece if d == 0 else 1 - piece) * n, n)
                go(ref, ref, y_send.at[i, piece, d], y_recv.at[i, piece, d], ydev[d])

    def y_wait(i, piece):
        n = chunks[i][2] // 2
        for d in range(2):
            ref = a_ref(i, down if d == 0 else up, core, (piece if d == 0 else 1 - piece) * n, n)
            arrived(ref, y_send.at[i, piece, d], y_recv.at[i, piece, d], ydev[d])

    def y_forward(i):
        n = chunks[i][2] // 2
        for d in range(2):
            ref = a_ref(i, down if d == 0 else up, core, d * n, n)
            go(ref, ref, y_send.at[i, 2, d], y_recv.at[i, 2, d], ydev[d])

    def y_last(i):
        n = chunks[i][2] // 2
        for d in range(2):
            ref = a_ref(i, across, core, d * n, n)
            arrived(ref, y_send.at[i, 2, d], y_recv.at[i, 2, d], ydev[d])

    ys = [y, up, down, across]

    def sib_start(i, j):
        ref = a_ref(i, ys[j], core, 0, chunks[i][2])
        go(ref, ref, s_send.at[i, j], s_recv.at[i, j], sibling)

    def sib_wait(i, js=(0, 1, 2, 3)):
        for j in js:
            arrived(a_ref(i, ys[j], 1 - core, 0, chunks[i][2]), s_send.at[i, j], s_recv.at[i, j], sibling)

    nb = 2 * rows

    def blocks(i):
        def pick(*of):
            return jnp.where(i == 0, of[0], jnp.where(i == 1, of[1], jnp.where(i == 2, of[2], of[3])))

        def block(along_z, along_x, second):
            bz, bx = z + along_z * (mz - z), x + along_x * (mx - x)
            return (bz + second * (pair(bz) - bz)) * 2 + bx // 2

        return [
            block(pick(0, 1, 0, 1), pick(0, 0, 1, 1), pick(0, 0, 1, 0)),
            block(pick(0, 0, 1, 1), pick(1, 0, 0, 1), pick(0, 1, 1, 1)),
        ]

    def dot(a, w):
        return lax.dot_general(a, w, (((1,), (1,)), ((), ())), preferred_element_type=F32)

    def product(o, t0, nt, ns, lo=0, hi=width):
        w = [wbuf[n // 2, pl.ds(2 * lax.rem(n, 2), 2), :, lo:hi].reshape(nb, hi - lo) for n in ns]
        a = [abuf[o, k, pl.ds(t0, nt), :] for k in range(lo // kh, hi // kh)]
        return dot(jnp.concatenate(a, axis=1), w[0] if len(w) == 1 else jnp.concatenate(w, axis=0))

    def out_copy(g, n):
        ts = pl.ds(*groups[g])
        return copy(obuf.at[n, ts, :], ibuf.at[n, ts, :], o_send.at[g, n], o_recv.at[g, n], pz_dev if g == 0 else px_dev)

    def nbr_product(g, ns):
        v = product(1, *groups[g], ns).astype(BF16)
        for j, n in enumerate(ns):
            obuf[n, pl.ds(*groups[g]), :] = v[:, j * nb:(j + 1) * nb]
        for n in ns:
            out_copy(g, n).start()

    def own_product(t0, nt, ns):
        v = product(0, t0, nt, ns)
        for j, n in enumerate(ns):
            ts = pl.ds(t0, nt)
            at = pl.ds(pl.multiple_of(n * nb, nb), nb)
            acc[n, ts, :] = v[:, j * nb:(j + 1) * nb] + resv[ts, at].astype(F32)

    def finish(n, t0, nt):
        ts = pl.ds(t0, nt)
        hid = (acc[n, ts, :] + ibuf[n, ts, :].astype(F32)).astype(BF16)
        hidden_o[ts, pl.ds(pl.multiple_of(n * nb, nb), nb)] = hid
        wide = hid.astype(F32)
        squares[ts, :] += wide * wide

    zero = r // NR

    def each(lo, hi, f):
        pl.loop(zero + lo, zero + hi)(f)

    for p in range(2):
        for k in range(NR):
            loads["w", p, k].wait()
        mate_start(0, p)
        if p == 0:
            nbr_start(0)
            loads["a"].wait()
            y_start(0)
    for p in range(2):
        for k in range(NR):
            loads["v", p, k].wait()
        pair_start(1, p)
        pair_start(2, p)
    sib_start(0, 0)
    y_wait(0, 0)
    y_forward(0)
    pair_wait(1, 0)
    mate_start(1, 0)
    nbr_start(1)
    y_wait(0, 1)
    sib_start(0, 1)
    sib_start(0, 2)
    pair_wait(1, 1)
    mate_start(1, 1)
    nbr_wait(0)
    y_start(1)
    sib_start(1, 0)
    y_last(0)
    sib_start(0, 3)
    pair_wait(2, 0)
    mate_start(2, 0)
    y_wait(1, 0)
    y_forward(1)
    pair_wait(2, 1)
    pl.semaphore_signal(gate, inc=1, device_id=diag_dev, device_id_type=MESH)
    mate_start(2, 1)
    nbr_wait(1)
    y_start(2)
    sib_start(2, 0)
    y_wait(1, 1)
    sib_start(1, 1)
    sib_start(1, 2)
    pl.semaphore_wait(gate, 1)
    pair_start(3, 0)
    pair_start(3, 1)
    sib_wait(0)
    loads["res"].wait()
    for s in range(2):
        for l in range(2):
            for p in range(2):
                mate_wait(l, s, p)
    each(0, 1, lambda i: own_product(0, t1, blocks(i)))
    pair_wait(3, 0)
    mate_start(3, 0)
    y_last(1)
    sib_start(1, 3)
    sib_wait(1)
    each(0, 1, lambda i: nbr_product(0, blocks(i)))
    pair_wait(3, 1)
    mate_start(3, 1)
    forward_start(0)
    forward_start(1)
    y_wait(2, 0)
    y_forward(2)
    y_start(3)
    sib_start(3, 0)
    each(1, 2, lambda i: nbr_product(0, blocks(i)))
    each(1, 2, lambda i: own_product(0, t1, blocks(i)))
    for l in range(2):
        for p in range(2):
            mate_wait(l, 2, p)
    forward_start(2)
    y_wait(2, 1)
    sib_start(2, 1)
    sib_start(2, 2)
    for l in range(2):
        for p in range(2):
            mate_wait(l, 3, p)
    for j in range(3, 6):
        forward_start(j)
    each(2, 3, lambda i: nbr_product(0, blocks(i)))
    y_last(2)
    sib_start(2, 3)
    sib_wait(2)
    each(0, 2, lambda i: nbr_product(1, blocks(i)))
    y_wait(3, 0)
    y_forward(3)
    y_start(4)
    sib_start(4, 0)
    each(2, 3, lambda i: nbr_product(1, blocks(i)))
    each(2, 3, lambda i: own_product(0, t1, blocks(i)))
    y_wait(3, 1)
    sib_start(3, 1)
    sib_start(3, 2)
    squares[...] = jnp.zeros_like(squares)

    @pl.loop(0, 3)
    def _(i):
        for n in blocks(i):
            out_copy(0, n).wait_recv()
            finish(n, 0, t1)

    forward_wait(0)
    forward_wait(1)
    first, last = blocks(3)

    @pl.loop(0, 2)
    def _(h):
        ts = pl.ds(pl.multiple_of(h * ht, ht), ht)
        obuf[first, ts, :] = product(1, ts.start, ht, [first]).astype(BF16)

    for h in range(2):
        out_copy(h, first).start()
    y_last(3)
    sib_start(3, 3)
    sib_wait(3)
    each(0, 1, lambda i: own_product(t1, t2 - t1, blocks(i)))
    y_wait(4, 0)
    y_forward(4)
    each(1, 3, lambda i: own_product(t1, t2 - t1, blocks(i)))
    forward_wait(2)
    forward_wait(3)

    @pl.loop(0, 2)
    def _(h):
        ts = pl.ds(pl.multiple_of(h * ht, ht), ht)
        early[ts, :] = product(1, ts.start, ht, [last], 0, late)

    y_wait(4, 1)
    sib_start(4, 1)
    sib_start(4, 2)
    forward_wait(4)
    forward_wait(5)

    @pl.loop(0, 2)
    def _(h):
        ts = pl.ds(pl.multiple_of(h * ht, ht), ht)
        obuf[last, ts, :] = (early[ts, :] + product(1, ts.start, ht, [last], late, width)).astype(BF16)

    for h in range(2):
        out_copy(h, last).start()
    y_last(4)
    sib_start(4, 3)
    pl.loop(0, 2)(lambda i: own_product(pl.multiple_of(i * t1, t1), t1, [first, last]))
    sib_wait(4)
    pl.loop(0, 2)(lambda i: own_product(t2, tokens - t2, blocks(2 * i) + blocks(2 * i + 1)))

    served = pltpu.make_async_copy(
        wbuf.at[:, :, :, pl.ds(pl.multiple_of((c // 2) * kh, kh), kh)], served_o, l_sem.at[len(loads)])
    served.start()

    @pl.loop(0, 3)
    def _(i):
        for n in blocks(i):
            out_copy(1, n).wait_recv()
            finish(n, t1, tokens - t1)

    for n in (first, last):
        for g in range(2):
            out_copy(g, n).wait_recv()
        finish(n, 0, tokens)

    for t in range(tokens // 128):
        sums[r, t:t + 1, :] = jnp.sum(squares[t * 128:(t + 1) * 128, :].T, axis=0, keepdims=True)
    for i, d in enumerate(peers):
        go(sums.at[r], sums.at[r], q_send.at[i], q_recv.at[i], d)
    for i in range(1, NR):
        arrived(sums.at[lax.rem(r + NR - i, NR)], q_send.at[i - 1], q_recv.at[i - 1], peers[i - 1])
    total = sums[0]
    for i in range(1, NR):
        total = total + sums[i]
    total_o[...] = total
    served.wait()
    for n in range(NR):
        for h in range(2):
            out_copy(h, n).wait_send()
    for cp in sent:
        cp.wait_send()


def finish(served, hidden, total, gain, served_o, hidden_o, normed_o, normv, sem):
    tokens, kw = hidden.shape
    copies = [
        pltpu.make_async_copy(hidden, hidden_o, sem.at[0]),
        pltpu.make_async_copy(served, served_o, sem.at[1]),
    ]
    for cp in copies:
        cp.start()
    inv = lax.rsqrt(total[...] / (NR * kw) + 1e-05)
    g = gain[...].astype(F32)[None, :]
    for t in range(tokens // 128):
        ts = slice(t * 128, (t + 1) * 128)
        scale = jnp.broadcast_to(inv[t:t + 1, :], (128, 128)).T
        for i in range(kw // 128):
            ls = slice(i * 128, (i + 1) * 128)
            normv[ts, ls] = (hidden[ts, ls].astype(F32) * scale * g[:, ls]).astype(BF16)
        cp = pltpu.make_async_copy(normv.at[ts, :], normed_o.at[ts, :], sem.at[2 + t])
        cp.start()
        copies.append(cp)
    for cp in copies:
        cp.wait()


def per_device(attention_out, residual, trainer_shard, norm_gain):
    tokens, kw = attention_out.shape
    rows, width = trainer_shard.shape
    kh = kw // 2
    hbm = pl.BlockSpec(memory_space=pltpu.HBM)
    vmem = pl.BlockSpec(memory_space=pltpu.VMEM)
    dma = pltpu.SemaphoreType.DMA
    shapes = (
        jax.ShapeDtypeStruct((NX, NX, rows, kw // 2), BF16),
        jax.ShapeDtypeStruct((tokens, kw), BF16),
        jax.ShapeDtypeStruct((tokens, kw), BF16),
    )
    served, hidden, total = pl.pallas_call(
        kernel,
        out_shape=tuple(pltpu.VMEM(a.shape, a.dtype) for a in shapes[:2]) + (pltpu.VMEM((tokens // 128, 128), F32),),
        in_specs=[hbm] * 3,
        out_specs=(vmem,) * 3,
        scratch_shapes=[
            pltpu.VMEM((NX, NX, rows, NR * kh), BF16),
            pltpu.VMEM((rows, NR * kh), BF16),
            pltpu.VMEM((2, NR, tokens, kh), BF16),
            pltpu.VMEM((NR, tokens, 2 * rows), F32),
            pltpu.VMEM((NR, tokens, 2 * rows), BF16),
            pltpu.VMEM((NR, tokens, 2 * rows), BF16),
            pltpu.VMEM((tokens, kw), BF16),
            pltpu.VMEM((tokens, 2 * rows), F32),
            pltpu.VMEM((tokens, 128), F32),
            pltpu.VMEM((NR, tokens // 128, 128), F32),
            dma((2, 14)), dma((2, 14)),
            dma((3, 2)), dma((3, 2)),
            dma((2,)), dma((2,)),
            dma((5, 3, 2)), dma((5, 3, 2)),
            dma((5, 4)), dma((5, 4)),
            dma((2, NR)), dma((2, NR)),
            dma((NR - 1,)), dma((NR - 1,)),
            dma((4 * NR + 3,)),
            pltpu.SemaphoreType.REGULAR,
        ],
        compiler_params=pltpu.CompilerParams(
            collective_id=0, has_side_effects=True, vmem_limit_bytes=50 * 1024 * 1024
        ),
        cost_estimate=pl.CostEstimate(
            flops=2 * tokens * kw * width, bytes_accessed=10 * tokens * kw, transcendentals=0
        ),
    )(attention_out, residual, trainer_shard)
    served, hidden, normed = pl.pallas_call(
        finish,
        out_shape=shapes,
        in_specs=[vmem] * 4,
        out_specs=(hbm,) * 3,
        scratch_shapes=[pltpu.VMEM((tokens, kw), BF16), dma((2 + tokens // 128,))],
        compiler_params=pltpu.CompilerParams(vmem_limit_bytes=16 * 1024 * 1024),
        cost_estimate=pl.CostEstimate(
            flops=4 * tokens * kw, bytes_accessed=5 * tokens * kw, transcendentals=tokens
        ),
    )(served, hidden, total, norm_gain)
    return (served.reshape(NX * NX * rows, kw // 2), hidden, normed)


def solution(mesh):
    in_specs = (P("col", "row"), P("col", "row"), P(("row", "col"), None), P("row"))
    out_specs = (P("row", "col"), P("col", "row"), P("col", "row"))
    return jax.shard_map(
        per_device, mesh=mesh, in_specs=in_specs, out_specs=out_specs, check_vma=False
    )
```

```python
import functools

import jax
import jax.numpy as jnp
from jax import lax
from jax.experimental import pallas as pl
from jax.experimental.pallas import tpu as pltpu
from jax.sharding import PartitionSpec as P

MESH = pl.DeviceIdType.MESH
NX = 4
NR = 8
F32 = jnp.float32
BF16 = jnp.bfloat16


def level(v):
    return lax.rem(v + v // 2, 2)


def pair(v):
    return v + 1 - 2 * lax.rem(v, 2)


def mate(v):
    return NX - 1 - v


def kernel(
    att, res, wsh,
    served_o, hidden_o, total_o,
    wbuf, wother, abuf, acc, obuf, ibuf, resv, early, squares, sums,
    c_send, c_recv, p_send, p_recv, n_send, n_recv, y_send, y_recv, s_send, s_recv, o_send, o_recv, q_send, q_recv, l_sem, gate,
):
    rows, kh = wsh.shape[0], abuf.shape[3]
    kw, tokens = 2 * kh, abuf.shape[2]
    part, ht = rows // 2, tokens // 2
    width = NR * kh
    late = 3 * width // 4
    r, c = lax.axis_index("row"), lax.axis_index("col")
    y, core = r // 2, lax.rem(r, 2)
    z, x = c // NX, lax.rem(c, NX)
    px, pz, mx, mz = pair(x), pair(z), mate(x), mate(z)
    colour = lax.rem(level(x) + level(z), 2)
    up, down, across = lax.rem(y + 1, NX), lax.rem(y + NX - 1, NX), lax.rem(y + 2, NX)

    px_dev, pz_dev, diag_dev = (r, z * NX + px), (r, pz * NX + x), (r, pz * NX + px)
    mates = [(r, z * NX + mx), (r, mz * NX + x)]
    ydev = [(up * 2 + core, c), (down * 2 + core, c)]
    sibling = (y * 2 + 1 - core, c)
    peers = [(lax.rem(r + i, NR), c) for i in range(1, NR)]

    barrier = pltpu.get_barrier_semaphore()
    greeted = [px_dev, pz_dev, diag_dev] + mates + peers
    for d in greeted:
        pl.semaphore_signal(barrier, inc=1, device_id=d, device_id_type=MESH)

    def cols(k, col):
        b = lax.rem(col + lax.rem(k, 2) + level(k // 2), 2)
        return pl.ds(pl.multiple_of(k * kw + b * kh, kh), kh)

    def my_cols(col):
        b = lax.rem(col + core + level(y), 2)
        return pl.ds(pl.multiple_of(b * kh, kh), kh)

    def load(src, dst, i):
        pltpu.make_async_copy(src, dst, l_sem.at[i]).start()

    def load_wait(ref, i):
        pltpu.make_async_copy(ref, ref, l_sem.at[i]).wait()

    def load_waits(ref, i):
        for k in range(NR):
            load_wait(ref.at[:, pl.ds(k * kh, kh)], 7 + i * NR + k)

    for p in range(2):
        for k in range(NR):
            ps, ks = pl.ds(p * part, part), pl.ds(k * kh, kh)
            load(wsh.at[ps, cols(k, colour)], wbuf.at[z, x, ps, ks], 7 + p * NR + k)
    for p in range(2):
        for k in range(NR):
            ps, ks = pl.ds(p * part, part), pl.ds(k * kh, kh)
            load(wsh.at[ps, cols(k, 1 - colour)], wother.at[ps, ks], 7 + (2 + p) * NR + k)
    load(att.at[:, my_cols(colour)], abuf.at[0, r], 4)
    load(res, resv, 5)
    pl.semaphore_wait(barrier, len(greeted))

    def copy(src, dst, ss, rs, d):
        return pltpu.make_async_remote_copy(
            src_ref=src, dst_ref=dst, send_sem=ss, recv_sem=rs, device_id=d, device_id_type=MESH
        )

    def go(src, dst, ss, rs, d):
        copy(src, dst, ss, rs, d).start()

    def arrived(ref, ss, rs):
        copy(ref, ref, ss, rs, sibling).wait_recv()

    def left(ref, ss, rs):
        copy(ref, ref, ss, rs, sibling).wait_send()

    def source(at_z, at_x, s):
        return (pair(at_z) if s >= 2 else at_z), (pair(at_x) if s % 2 else at_x)

    def w_ref(at_z, at_x, s, p, lo=0, hi=width):
        sz, sx = source(at_z, at_x, s)
        return wbuf.at[sz, sx, pl.ds(p * part, part), pl.ds(lo, hi - lo)]

    def pair_start(s, p):
        ps = pl.ds(p * part, part)
        src = wbuf.at[z, x, ps, :] if s == 3 else wother.at[ps, :]
        d = [px_dev, pz_dev, diag_dev][s - 1]
        go(src, wbuf.at[z, x, ps, :], p_send, p_recv.at[s - 1, p], d)

    def pair_wait(s, p):
        arrived(w_ref(z, x, s, p), p_send, p_recv.at[s - 1, p])

    def mate_start(s, p):
        for l in range(2):
            ref = w_ref(z, x, s, p)
            go(ref, ref, c_send, c_recv.at[l, 2 * s + p], mates[l])

    def mate_wait(i):
        for s in ((0, 1), (2,), (3,))[i]:
            for p in range(2):
                arrived(w_ref(z, mx, s, p), c_send, c_recv.at[0, 2 * s + p])
                arrived(w_ref(mz, x, s, p), c_send, c_recv.at[1, 2 * s + p])

    pieces = [(0, 0, width), (1, 0, width), (2, 0, late), (3, 0, late), (2, late, width), (3, late, width)]

    def forward_start(j):
        s, lo, hi = pieces[j]
        ref = w_ref(z, mx, s, 0, lo, hi)
        go(ref, ref, c_send, c_recv.at[1, 8 + j], mates[1])
        ref = w_ref(mz, x, s, 1, lo, hi)
        go(ref, ref, c_send, c_recv.at[0, 8 + j], mates[0])

    def forward_wait(i):
        for j in (2 * i, 2 * i + 1):
            s, lo, hi = pieces[j]
            for l in range(2):
                arrived(w_ref(mz, mx, s, 1 - l, lo, hi), c_send, c_recv.at[l, 8 + j])

    t1, t2 = 3 * tokens // 8, 6 * tokens // 8
    groups = [(0, 8 * tokens // 16), (8 * tokens // 16, 8 * tokens // 16)]
    chunks = [(0, 0, t1), (1, *groups[0]), (1, *groups[1]), (0, t1, t2 - t1), (0, t2, tokens - t2)]

    def a_ref(i, at_y, k, lo, n):
        o, t0, _ = chunks[i]
        return abuf.at[o, at_y * 2 + k, pl.ds(t0 + lo, n), :]

    def nbr_ref(g):
        return abuf.at[1, r, pl.ds(*groups[g]), :]

    def nbr_start(g):
        src = att.at[pl.ds(*groups[g]), my_cols(1 - colour)]
        go(src, nbr_ref(g), n_send, n_recv.at[g], pz_dev if g == 0 else px_dev)

    def nbr_wait(g):
        arrived(nbr_ref(g), n_send, n_recv.at[g])

    def y_start(i):
        n = chunks[i][2] // 2
        for piece in range(2):
            for d in range(2):
                ref = a_ref(i, y, core, (piece if d == 0 else 1 - piece) * n, n)
                go(ref, ref, y_send, y_recv.at[i, piece, d], ydev[d])

    def y_wait(i, piece):
        n = chunks[i][2] // 2
        for d in range(2):
            ref = a_ref(i, down if d == 0 else up, core, (piece if d == 0 else 1 - piece) * n, n)
            arrived(ref, y_send, y_recv.at[i, piece, d])

    def y_forward(i):
        n = chunks[i][2] // 2
        for d in range(2):
            ref = a_ref(i, down if d == 0 else up, core, d * n, n)
            go(ref, ref, y_send, y_recv.at[i, 2, d], ydev[d])

    def y_last(i):
        n = chunks[i][2] // 2
        for d in range(2):
            arrived(a_ref(i, across, core, d * n, n), y_send, y_recv.at[i, 2, d])

    ys = [y, up, down, across]

    def sib_start(i, j):
        ref = a_ref(i, ys[j], core, 0, chunks[i][2])
        go(ref, ref, s_send, s_recv.at[i, j], sibling)

    def sib_wait(i):
        for j in range(4):
            arrived(a_ref(i, ys[j], 1 - core, 0, chunks[i][2]), s_send, s_recv.at[i, j])

    nb = 2 * rows

    def blocks(i):
        def pick(*of):
            return jnp.where(i == 0, of[0], jnp.where(i == 1, of[1], jnp.where(i == 2, of[2], of[3])))

        def block(along_z, along_x, second):
            bz, bx = z + along_z * (mz - z), x + along_x * (mx - x)
            return (bz + second * (pair(bz) - bz)) * 2 + bx // 2

        return [
            block(pick(0, 1, 0, 1), pick(0, 0, 1, 1), pick(0, 0, 1, 0)),
            block(pick(0, 0, 1, 1), pick(1, 0, 0, 1), pick(0, 1, 1, 1)),
        ]

    def dot(a, w):
        return lax.dot_general(a, w, (((1,), (1,)), ((), ())), preferred_element_type=F32)

    def product(o, t0, nt, ns, lo=0, hi=width):
        w = [wbuf[n // 2, pl.ds(2 * lax.rem(n, 2), 2), :, lo:hi].reshape(nb, hi - lo) for n in ns]
        a = [abuf[o, k, pl.ds(t0, nt), :] for k in range(lo // kh, hi // kh)]
        return dot(jnp.concatenate(a, axis=1), w[0] if len(w) == 1 else jnp.concatenate(w, axis=0))

    def out_start(g, n):
        ts = pl.ds(*groups[g])
        go(obuf.at[n, ts, :], ibuf.at[n, ts, :], o_send, o_recv.at[g, n], pz_dev if g == 0 else px_dev)

    def out_wait(g, n):
        arrived(ibuf.at[n, pl.ds(*groups[g]), :], o_send, o_recv.at[g, n])

    def nbr_product(g, ns):
        v = product(1, *groups[g], ns).astype(BF16)
        for j, n in enumerate(ns):
            obuf[n, pl.ds(*groups[g]), :] = v[:, j * nb:(j + 1) * nb]
        for n in ns:
            out_start(g, n)

    def own_product(t0, nt, ns):
        v = product(0, t0, nt, ns)
        for j, n in enumerate(ns):
            ts = pl.ds(t0, nt)
            at = pl.ds(pl.multiple_of(n * nb, nb), nb)
            acc[n, ts, :] = v[:, j * nb:(j + 1) * nb] + resv[ts, at].astype(F32)

    def finish(n, t0, nt):
        ts = pl.ds(t0, nt)
        hid = (acc[n, ts, :] + ibuf[n, ts, :].astype(F32)).astype(BF16)
        hidden_o[ts, pl.ds(pl.multiple_of(n * nb, nb), nb)] = hid
        wide = hid.astype(F32)
        squares[ts, :] += wide * wide

    zero = r // NR

    def each(lo, hi, f):
        pl.loop(zero + lo, zero + hi)(f)

    for p in range(2):
        load_waits(wbuf.at[z, x, pl.ds(p * part, part), :], p)
        mate_start(0, p)
        if p == 0:
            nbr_start(0)
            load_wait(abuf.at[0, r], 4)
            y_start(0)
    for p in range(2):
        load_waits(wother.at[pl.ds(p * part, part), :], 2 + p)
        pair_start(1, p)
        pair_start(2, p)
    sib_start(0, 0)
    y_wait(0, 0)
    y_forward(0)
    pair_wait(1, 0)
    mate_start(1, 0)
    nbr_start(1)
    y_wait(0, 1)
    sib_start(0, 1)
    sib_start(0, 2)
    pair_wait(1, 1)
    mate_start(1, 1)
    nbr_wait(0)
    y_start(1)
    sib_start(1, 0)
    y_last(0)
    sib_start(0, 3)
    pair_wait(2, 0)
    mate_start(2, 0)
    y_wait(1, 0)
    y_forward(1)
    pair_wait(2, 1)
    pl.semaphore_signal(gate, inc=1, device_id=diag_dev, device_id_type=MESH)
    mate_start(2, 1)
    nbr_wait(1)
    y_start(2)
    sib_start(2, 0)
    y_wait(1, 1)
    sib_start(1, 1)
    sib_start(1, 2)
    pl.semaphore_wait(gate, 1)
    pair_start(3, 0)
    pair_start(3, 1)
    sib_wait(0)
    load_wait(resv, 5)
    mate_wait(0)
    each(0, 1, lambda i: own_product(0, t1, blocks(i)))
    pair_wait(3, 0)
    mate_start(3, 0)
    y_last(1)
    sib_start(1, 3)
    sib_wait(1)
    each(0, 1, lambda i: nbr_product(0, blocks(i)))
    pair_wait(3, 1)
    mate_start(3, 1)
    forward_start(0)
    forward_start(1)
    y_wait(2, 0)
    y_forward(2)
    y_start(3)
    sib_start(3, 0)
    each(1, 2, lambda i: nbr_product(0, blocks(i)))
    each(1, 2, lambda i: own_product(0, t1, blocks(i)))
    mate_wait(1)
    forward_start(2)
    y_wait(2, 1)
    sib_start(2, 1)
    sib_start(2, 2)
    mate_wait(2)
    for j in range(3, 6):
        forward_start(j)
    each(2, 3, lambda i: nbr_product(0, blocks(i)))
    y_last(2)
    sib_start(2, 3)
    sib_wait(2)
    each(0, 2, lambda i: nbr_product(1, blocks(i)))
    y_wait(3, 0)
    y_forward(3)
    y_start(4)
    sib_start(4, 0)
    each(2, 3, lambda i: nbr_product(1, blocks(i)))
    each(2, 3, lambda i: own_product(0, t1, blocks(i)))
    y_wait(3, 1)
    sib_start(3, 1)
    sib_start(3, 2)
    squares[...] = jnp.zeros_like(squares)

    @pl.loop(0, 3)
    def _(i):
        for n in blocks(i):
            out_wait(0, n)
            finish(n, 0, t1)

    forward_wait(0)
    first, last = blocks(3)

    @pl.loop(0, 2)
    def _(h):
        ts = pl.ds(pl.multiple_of(h * ht, ht), ht)
        obuf[first, ts, :] = product(1, ts.start, ht, [first]).astype(BF16)

    for g in range(2):
        out_start(g, first)
    y_last(3)
    sib_start(3, 3)
    sib_wait(3)
    each(0, 1, lambda i: own_product(t1, t2 - t1, blocks(i)))
    y_wait(4, 0)
    y_forward(4)
    each(1, 3, lambda i: own_product(t1, t2 - t1, blocks(i)))
    forward_wait(1)

    @pl.loop(0, 2)
    def _(h):
        ts = pl.ds(pl.multiple_of(h * ht, ht), ht)
        early[ts, :] = product(1, ts.start, ht, [last], 0, late)

    y_wait(4, 1)
    sib_start(4, 1)
    sib_start(4, 2)
    forward_wait(2)

    @pl.loop(0, 2)
    def _(h):
        ts = pl.ds(pl.multiple_of(h * ht, ht), ht)
        obuf[last, ts, :] = (early[ts, :] + product(1, ts.start, ht, [last], late, width)).astype(BF16)

    for g in range(2):
        out_start(g, last)
    y_last(4)
    sib_start(4, 3)
    @pl.loop(0, 2)
    def _(i):
        own_product(pl.multiple_of(i * t1, t1), t1, [first, last])
        for j in range(3):
            k = 3 * i + j
            one, other = blocks(k // 2)
            n = jnp.where(lax.rem(k, 2) == 0, one, other)
            out_wait(1, n)
            finish(n, t1, t2 - t1)

    sib_wait(4)
    pl.loop(0, 2)(lambda i: own_product(t2, tokens - t2, blocks(2 * i) + blocks(2 * i + 1)))

    served = pltpu.make_async_copy(
        wbuf.at[:, :, :, pl.ds(pl.multiple_of((c // 2) * kh, kh), kh)], served_o, l_sem.at[6])
    served.start()

    @pl.loop(0, 3)
    def _(i):
        for n in blocks(i):
            finish(n, t2, tokens - t2)

    for n in (first, last):
        for g in range(2):
            out_wait(g, n)
        finish(n, 0, tokens)

    for t in range(tokens // 128):
        sums[r, t:t + 1, :] = jnp.sum(squares[t * 128:(t + 1) * 128, :].T, axis=0, keepdims=True)
    for i in (3, 4, 2, 5, 1, 6, 0):
        go(sums.at[r], sums.at[r], q_send, q_recv.at[i], peers[i])
    served.wait()
    left(wbuf.at[pl.ds(0, 3)], c_send, c_recv.at[0, 0])
    left(wbuf.at[0, pl.ds(0, 3)], p_send, p_recv.at[0, 0])
    left(abuf.at[0, 0], n_send, n_recv.at[0])
    left(abuf.at[0, pl.ds(0, 6)], y_send, y_recv.at[0, 0, 0])
    left(abuf.at[0], s_send, s_recv.at[0, 0])
    left(obuf, o_send, o_recv.at[0, 0])
    for i in range(1, NR):
        arrived(sums.at[lax.rem(r + NR - i, NR)], q_send, q_recv.at[i - 1])
    total = sums[0]
    for i in range(1, NR):
        total = total + sums[i]
    total_o[...] = total
    left(sums.at[pl.ds(0, NR - 1)], q_send, q_recv.at[0])


def finish(served, hidden, total, gain, served_o, hidden_o, normed_o, normv, sem):
    tokens, kw = hidden.shape
    copies = [
        pltpu.make_async_copy(hidden, hidden_o, sem.at[0]),
        pltpu.make_async_copy(served, served_o, sem.at[1]),
    ]
    for cp in copies:
        cp.start()
    inv = lax.rsqrt(total[...] / (NR * kw) + 1e-05)
    g = gain[...].astype(F32)[None, :]
    for t in range(tokens // 128):
        ts = slice(t * 128, (t + 1) * 128)
        scale = jnp.broadcast_to(inv[t:t + 1, :], (128, 128)).T
        for i in range(kw // 128):
            ls = slice(i * 128, (i + 1) * 128)
            normv[ts, ls] = (hidden[ts, ls].astype(F32) * scale * g[:, ls]).astype(BF16)
        cp = pltpu.make_async_copy(normv.at[ts, :], normed_o.at[ts, :], sem.at[2 + t])
        cp.start()
        copies.append(cp)
    for cp in copies:
        cp.wait()


def per_device(attention_out, residual, trainer_shard, norm_gain):
    tokens, kw = attention_out.shape
    rows, width = trainer_shard.shape
    kh = kw // 2
    hbm = pl.BlockSpec(memory_space=pltpu.HBM)
    vmem = pl.BlockSpec(memory_space=pltpu.VMEM)
    dma = pltpu.SemaphoreType.DMA
    shapes = (
        jax.ShapeDtypeStruct((NX, NX, rows, kw // 2), BF16),
        jax.ShapeDtypeStruct((tokens, kw), BF16),
        jax.ShapeDtypeStruct((tokens, kw), BF16),
    )
    served, hidden, total = pl.pallas_call(
        kernel,
        out_shape=tuple(pltpu.VMEM(a.shape, a.dtype) for a in shapes[:2]) + (pltpu.VMEM((tokens // 128, 128), F32),),
        in_specs=[hbm] * 3,
        out_specs=(vmem,) * 3,
        scratch_shapes=[
            pltpu.VMEM((NX, NX, rows, NR * kh), BF16),
            pltpu.VMEM((rows, NR * kh), BF16),
            pltpu.VMEM((2, NR, tokens, kh), BF16),
            pltpu.VMEM((NR, tokens, 2 * rows), F32),
            pltpu.VMEM((NR, tokens, 2 * rows), BF16),
            pltpu.VMEM((NR, tokens, 2 * rows), BF16),
            pltpu.VMEM((tokens, kw), BF16),
            pltpu.VMEM((tokens, 2 * rows), F32),
            pltpu.VMEM((tokens, 128), F32),
            pltpu.VMEM((NR, tokens // 128, 128), F32),
            dma(()), dma((2, 14)),
            dma(()), dma((3, 2)),
            dma(()), dma((2,)),
            dma(()), dma((5, 3, 2)),
            dma(()), dma((5, 4)),
            dma(()), dma((2, NR)),
            dma(()), dma((NR - 1,)),
            dma((7 + 4 * NR,)),
            pltpu.SemaphoreType.REGULAR,
        ],
        compiler_params=pltpu.CompilerParams(
            collective_id=0, has_side_effects=True, vmem_limit_bytes=50 * 1024 * 1024
        ),
        cost_estimate=pl.CostEstimate(
            flops=2 * tokens * kw * width, bytes_accessed=10 * tokens * kw, transcendentals=0
        ),
    )(attention_out, residual, trainer_shard)
    served, hidden, normed = pl.pallas_call(
        finish,
        out_shape=shapes,
        in_specs=[vmem] * 4,
        out_specs=(hbm,) * 3,
        scratch_shapes=[pltpu.VMEM((tokens, kw), BF16), dma((2 + tokens // 128,))],
        compiler_params=pltpu.CompilerParams(vmem_limit_bytes=16 * 1024 * 1024),
        cost_estimate=pl.CostEstimate(
            flops=4 * tokens * kw, bytes_accessed=5 * tokens * kw, transcendentals=tokens
        ),
    )(served, hidden, total, norm_gain)
    return (served.reshape(NX * NX * rows, kw // 2), hidden, normed)


def solution(mesh):
    in_specs = (P("col", "row"), P("col", "row"), P(("row", "col"), None), P("row"))
    out_specs = (P("row", "col"), P("col", "row"), P("col", "row"))
    return jax.shard_map(
        per_device, mesh=mesh, in_specs=in_specs, out_specs=out_specs, check_vma=False
    )
```

```python
import functools

import jax
import jax.numpy as jnp
from jax import lax
from jax.experimental import pallas as pl
from jax.experimental.pallas import tpu as pltpu
from jax.sharding import PartitionSpec as P

MESH = pl.DeviceIdType.MESH
NX = 4
NR = 8
F32 = jnp.float32
BF16 = jnp.bfloat16


def level(v):
    return lax.rem(v + v // 2, 2)


def pair(v):
    return v + 1 - 2 * lax.rem(v, 2)


def mate(v):
    return NX - 1 - v


def kernel(
    att, res, wsh,
    served_o, hidden_o, total_o,
    wbuf, wother, abuf, acc, obuf, ibuf, resv, early, squares, sums,
    c_send, c_recv, p_send, p_recv, n_send, n_recv, y_send, y_recv, s_send, s_recv, o_send, o_recv, q_send, q_recv, l_sem, gate,
):
    rows, kh = wsh.shape[0], abuf.shape[3]
    kw, tokens = 2 * kh, abuf.shape[2]
    part, ht = rows // 2, tokens // 2
    width = NR * kh
    late = 3 * width // 4
    r, c = lax.axis_index("row"), lax.axis_index("col")
    y, core = r // 2, lax.rem(r, 2)
    z, x = c // NX, lax.rem(c, NX)
    px, pz, mx, mz = pair(x), pair(z), mate(x), mate(z)
    colour = lax.rem(level(x) + level(z), 2)
    up, down, across = lax.rem(y + 1, NX), lax.rem(y + NX - 1, NX), lax.rem(y + 2, NX)

    px_dev, pz_dev, diag_dev = (r, z * NX + px), (r, pz * NX + x), (r, pz * NX + px)
    mates = [(r, z * NX + mx), (r, mz * NX + x)]
    ydev = [(up * 2 + core, c), (down * 2 + core, c)]
    sibling = (y * 2 + 1 - core, c)
    peers = [(lax.rem(r + i, NR), c) for i in range(1, NR)]

    barrier = pltpu.get_barrier_semaphore()
    greeted = [px_dev, pz_dev, diag_dev] + mates + peers
    for d in greeted:
        pl.semaphore_signal(barrier, inc=1, device_id=d, device_id_type=MESH)

    def cols(k, col):
        b = lax.rem(col + lax.rem(k, 2) + level(k // 2), 2)
        return pl.ds(pl.multiple_of(k * kw + b * kh, kh), kh)

    def my_cols(col):
        b = lax.rem(col + core + level(y), 2)
        return pl.ds(pl.multiple_of(b * kh, kh), kh)

    def load(src, dst, i):
        pltpu.make_async_copy(src, dst, l_sem.at[i]).start()

    def load_wait(ref, i):
        pltpu.make_async_copy(ref, ref, l_sem.at[i]).wait()

    for p in range(2):
        for k in range(NR):
            ps, ks = pl.ds(p * part, part), pl.ds(k * kh, kh)
            load(wsh.at[ps, cols(k, colour)], wbuf.at[z, x, ps, ks], p)
    for p in range(2):
        for k in range(NR):
            ps, ks = pl.ds(p * part, part), pl.ds(k * kh, kh)
            load(wsh.at[ps, cols(k, 1 - colour)], wother.at[ps, ks], 2 + p)
    load(att.at[:, my_cols(colour)], abuf.at[0, r], 4)
    load(res, resv, 5)
    pl.semaphore_wait(barrier, len(greeted))

    def copy(src, dst, ss, rs, d):
        return pltpu.make_async_remote_copy(
            src_ref=src, dst_ref=dst, send_sem=ss, recv_sem=rs, device_id=d, device_id_type=MESH
        )

    def go(src, dst, ss, rs, d):
        copy(src, dst, ss, rs, d).start()

    def arrived(ref, ss, rs):
        copy(ref, ref, ss, rs, sibling).wait_recv()

    def left(ref, ss, rs):
        copy(ref, ref, ss, rs, sibling).wait_send()

    def source(at_z, at_x, s):
        return (pair(at_z) if s >= 2 else at_z), (pair(at_x) if s % 2 else at_x)

    def w_ref(at_z, at_x, s, p, lo=0, hi=width):
        sz, sx = source(at_z, at_x, s)
        return wbuf.at[sz, sx, pl.ds(p * part, part), pl.ds(lo, hi - lo)]

    def pair_start(s, p):
        ps = pl.ds(p * part, part)
        src = wbuf.at[z, x, ps, :] if s == 3 else wother.at[ps, :]
        d = [px_dev, pz_dev, diag_dev][s - 1]
        go(src, wbuf.at[z, x, ps, :], p_send, p_recv.at[s - 1, p], d)

    def pair_wait(s, p):
        arrived(w_ref(z, x, s, p), p_send, p_recv.at[s - 1, p])

    def mate_start(s, p):
        for l in range(2):
            ref = w_ref(z, x, s, p)
            go(ref, ref, c_send, c_recv.at[l, 2 * s + p], mates[l])

    def mate_wait(i):
        for s in ((0, 1), (2,), (3,))[i]:
            for p in range(2):
                arrived(w_ref(z, mx, s, p), c_send, c_recv.at[0, 2 * s + p])
                arrived(w_ref(mz, x, s, p), c_send, c_recv.at[1, 2 * s + p])

    pieces = [(0, 0, width), (1, 0, width), (2, 0, late), (3, 0, late), (2, late, width), (3, late, width)]

    def forward_start(j):
        s, lo, hi = pieces[j]
        ref = w_ref(z, mx, s, 0, lo, hi)
        go(ref, ref, c_send, c_recv.at[1, 8 + j], mates[1])
        ref = w_ref(mz, x, s, 1, lo, hi)
        go(ref, ref, c_send, c_recv.at[0, 8 + j], mates[0])

    def forward_wait(i):
        for j in (2 * i, 2 * i + 1):
            s, lo, hi = pieces[j]
            for l in range(2):
                arrived(w_ref(mz, mx, s, 1 - l, lo, hi), c_send, c_recv.at[l, 8 + j])

    t1, t2 = 3 * tokens // 8, 6 * tokens // 8
    groups = [(0, 8 * tokens // 16), (8 * tokens // 16, 8 * tokens // 16)]
    chunks = [(0, 0, t1), (1, *groups[0]), (1, *groups[1]), (0, t1, t2 - t1), (0, t2, tokens - t2)]

    def a_ref(i, at_y, k, lo, n):
        o, t0, _ = chunks[i]
        return abuf.at[o, at_y * 2 + k, pl.ds(t0 + lo, n), :]

    def nbr_ref(g):
        return abuf.at[1, r, pl.ds(*groups[g]), :]

    def nbr_start(g):
        src = att.at[pl.ds(*groups[g]), my_cols(1 - colour)]
        go(src, nbr_ref(g), n_send, n_recv.at[g], pz_dev if g == 0 else px_dev)

    def nbr_wait(g):
        arrived(nbr_ref(g), n_send, n_recv.at[g])

    def y_start(i):
        n = chunks[i][2] // 2
        for piece in range(2):
            for d in range(2):
                ref = a_ref(i, y, core, (piece if d == 0 else 1 - piece) * n, n)
                go(ref, ref, y_send, y_recv.at[i, piece], ydev[d])

    def y_wait(i, piece):
        arrived(a_ref(i, y, core, 0, chunks[i][2]), y_send, y_recv.at[i, piece])

    def y_forward(i):
        n = chunks[i][2] // 2
        for d in range(2):
            ref = a_ref(i, down if d == 0 else up, core, d * n, n)
            go(ref, ref, y_send, y_recv.at[i, 2], ydev[d])

    def y_last(i):
        y_wait(i, 2)

    ys = [y, up, down, across]

    def sib_start(i, j):
        ref = a_ref(i, ys[j], core, 0, chunks[i][2])
        go(ref, ref, s_send, s_recv.at[i], sibling)

    def sib_wait(i):
        o, t0, n = chunks[i]
        arrived(abuf.at[o, pl.ds(0, 4), pl.ds(t0, n), :], s_send, s_recv.at[i])

    nb = 2 * rows

    def blocks(i):
        def pick(*of):
            return jnp.where(i == 0, of[0], jnp.where(i == 1, of[1], jnp.where(i == 2, of[2], of[3])))

        def block(along_z, along_x, second):
            bz, bx = z + along_z * (mz - z), x + along_x * (mx - x)
            return (bz + second * (pair(bz) - bz)) * 2 + bx // 2

        return [
            block(pick(0, 1, 0, 1), pick(0, 0, 1, 1), pick(0, 0, 1, 0)),
            block(pick(0, 0, 1, 1), pick(1, 0, 0, 1), pick(0, 1, 1, 1)),
        ]

    def dot(a, w):
        return lax.dot_general(a, w, (((1,), (1,)), ((), ())), preferred_element_type=F32)

    def product(o, t0, nt, ns, lo=0, hi=width):
        w = [wbuf[n // 2, pl.ds(2 * lax.rem(n, 2), 2), :, lo:hi].reshape(nb, hi - lo) for n in ns]
        a = [abuf[o, k, pl.ds(t0, nt), :] for k in range(lo // kh, hi // kh)]
        return dot(jnp.concatenate(a, axis=1), w[0] if len(w) == 1 else jnp.concatenate(w, axis=0))

    def out_start(g, n):
        ts = pl.ds(*groups[g])
        go(obuf.at[n, ts, :], ibuf.at[n, ts, :], o_send, o_recv.at[g, n], pz_dev if g == 0 else px_dev)

    def out_wait(g, n):
        arrived(ibuf.at[n, pl.ds(*groups[g]), :], o_send, o_recv.at[g, n])

    def nbr_product(g, ns):
        v = product(1, *groups[g], ns).astype(BF16)
        for j, n in enumerate(ns):
            obuf[n, pl.ds(*groups[g]), :] = v[:, j * nb:(j + 1) * nb]
        for n in ns:
            out_start(g, n)

    def own_product(t0, nt, ns):
        v = product(0, t0, nt, ns)
        for j, n in enumerate(ns):
            ts = pl.ds(t0, nt)
            at = pl.ds(pl.multiple_of(n * nb, nb), nb)
            acc[n, ts, :] = v[:, j * nb:(j + 1) * nb] + resv[ts, at].astype(F32)

    def finish(n, t0, nt):
        ts = pl.ds(t0, nt)
        hid = (acc[n, ts, :] + ibuf[n, ts, :].astype(F32)).astype(BF16)
        hidden_o[ts, pl.ds(pl.multiple_of(n * nb, nb), nb)] = hid
        wide = hid.astype(F32)
        squares[ts, :] += wide * wide

    zero = r // NR

    def each(lo, hi, f):
        pl.loop(zero + lo, zero + hi)(f)

    for p in range(2):
        load_wait(wbuf.at[z, x, pl.ds(p * part, part), :], p)
        mate_start(0, p)
        if p == 0:
            nbr_start(0)
            load_wait(abuf.at[0, r], 4)
            y_start(0)
    for p in range(2):
        load_wait(wother.at[pl.ds(p * part, part), :], 2 + p)
        pair_start(1, p)
        pair_start(2, p)
    sib_start(0, 0)
    y_wait(0, 0)
    y_forward(0)
    pair_wait(1, 0)
    mate_start(1, 0)
    nbr_start(1)
    y_wait(0, 1)
    sib_start(0, 1)
    sib_start(0, 2)
    pair_wait(1, 1)
    mate_start(1, 1)
    nbr_wait(0)
    y_start(1)
    sib_start(1, 0)
    y_last(0)
    sib_start(0, 3)
    pair_wait(2, 0)
    mate_start(2, 0)
    y_wait(1, 0)
    y_forward(1)
    pair_wait(2, 1)
    pl.semaphore_signal(gate, inc=1, device_id=diag_dev, device_id_type=MESH)
    mate_start(2, 1)
    nbr_wait(1)
    y_start(2)
    sib_start(2, 0)
    y_wait(1, 1)
    sib_start(1, 1)
    sib_start(1, 2)
    pl.semaphore_wait(gate, 1)
    pair_start(3, 0)
    pair_start(3, 1)
    sib_wait(0)
    load_wait(resv, 5)
    mate_wait(0)
    each(0, 1, lambda i: own_product(0, t1, blocks(i)))
    pair_wait(3, 0)
    mate_start(3, 0)
    y_last(1)
    sib_start(1, 3)
    sib_wait(1)
    each(0, 1, lambda i: nbr_product(0, blocks(i)))
    pair_wait(3, 1)
    mate_start(3, 1)
    forward_start(0)
    forward_start(1)
    y_wait(2, 0)
    y_forward(2)
    y_start(3)
    sib_start(3, 0)
    each(1, 2, lambda i: nbr_product(0, blocks(i)))
    each(1, 2, lambda i: own_product(0, t1, blocks(i)))
    mate_wait(1)
    forward_start(2)
    y_wait(2, 1)
    sib_start(2, 1)
    sib_start(2, 2)
    mate_wait(2)
    for j in range(3, 6):
        forward_start(j)
    each(2, 3, lambda i: nbr_product(0, blocks(i)))
    y_last(2)
    sib_start(2, 3)
    sib_wait(2)
    each(0, 2, lambda i: nbr_product(1, blocks(i)))
    y_wait(3, 0)
    y_forward(3)
    y_start(4)
    sib_start(4, 0)
    each(2, 3, lambda i: nbr_product(1, blocks(i)))
    each(2, 3, lambda i: own_product(0, t1, blocks(i)))
    y_wait(3, 1)
    sib_start(3, 1)
    sib_start(3, 2)
    squares[...] = jnp.zeros_like(squares)

    @pl.loop(0, 3)
    def _(i):
        for n in blocks(i):
            out_wait(0, n)
            finish(n, 0, t1)

    forward_wait(0)
    first, last = blocks(3)

    @pl.loop(0, 2)
    def _(h):
        ts = pl.ds(pl.multiple_of(h * ht, ht), ht)
        obuf[first, ts, :] = product(1, ts.start, ht, [first]).astype(BF16)

    for g in range(2):
        out_start(g, first)
    y_last(3)
    sib_start(3, 3)
    sib_wait(3)
    each(0, 1, lambda i: own_product(t1, t2 - t1, blocks(i)))
    y_wait(4, 0)
    y_forward(4)
    each(1, 3, lambda i: own_product(t1, t2 - t1, blocks(i)))
    forward_wait(1)

    @pl.loop(0, 2)
    def _(h):
        ts = pl.ds(pl.multiple_of(h * ht, ht), ht)
        early[ts, :] = product(1, ts.start, ht, [last], 0, late)

    y_wait(4, 1)
    sib_start(4, 1)
    sib_start(4, 2)
    forward_wait(2)

    @pl.loop(0, 2)
    def _(h):
        ts = pl.ds(pl.multiple_of(h * ht, ht), ht)
        obuf[last, ts, :] = (early[ts, :] + product(1, ts.start, ht, [last], late, width)).astype(BF16)

    for g in range(2):
        out_start(g, last)
    y_last(4)
    sib_start(4, 3)
    @pl.loop(0, 2)
    def _(i):
        own_product(pl.multiple_of(i * t1, t1), t1, [first, last])
        for j in range(3):
            k = 3 * i + j
            one, other = blocks(k // 2)
            n = jnp.where(lax.rem(k, 2) == 0, one, other)
            out_wait(1, n)
            finish(n, t1, t2 - t1)

    sib_wait(4)
    pl.loop(0, 2)(lambda i: own_product(t2, tokens - t2, blocks(2 * i) + blocks(2 * i + 1)))

    served = pltpu.make_async_copy(
        wbuf.at[:, :, :, pl.ds(pl.multiple_of((c // 2) * kh, kh), kh)], served_o, l_sem.at[6])
    served.start()

    @pl.loop(0, 3)
    def _(i):
        for n in blocks(i):
            finish(n, t2, tokens - t2)

    for n in (first, last):
        for g in range(2):
            out_wait(g, n)
        finish(n, 0, tokens)

    for t in range(tokens // 128):
        sums[r, t:t + 1, :] = jnp.sum(squares[t * 128:(t + 1) * 128, :].T, axis=0, keepdims=True)
    for i in (3, 4, 2, 5, 1, 6, 0):
        go(sums.at[r], sums.at[r], q_send, q_recv, peers[i])
    served.wait()
    left(wbuf.at[pl.ds(0, 3)], c_send, c_recv.at[0, 0])
    left(wbuf.at[0, pl.ds(0, 3)], p_send, p_recv.at[0, 0])
    left(abuf.at[0, 0], n_send, n_recv.at[0])
    left(abuf.at[0, pl.ds(0, 6)], y_send, y_recv.at[0, 0])
    left(abuf.at[0], s_send, s_recv.at[0])
    left(obuf, o_send, o_recv.at[0, 0])
    arrived(sums.at[pl.ds(0, NR - 1)], q_send, q_recv)
    total = sums[0]
    for i in range(1, NR):
        total = total + sums[i]
    total_o[...] = total
    left(sums.at[pl.ds(0, NR - 1)], q_send, q_recv)


def finish(served, hidden, total, gain, served_o, hidden_o, normed_o, normv, sem):
    tokens, kw = hidden.shape
    copies = [
        pltpu.make_async_copy(hidden, hidden_o, sem.at[0]),
        pltpu.make_async_copy(served, served_o, sem.at[1]),
    ]
    for cp in copies:
        cp.start()
    inv = lax.rsqrt(total[...] / (NR * kw) + 1e-05)
    g = gain[...].astype(F32)[None, :]
    for t in range(tokens // 128):
        ts = slice(t * 128, (t + 1) * 128)
        scale = jnp.broadcast_to(inv[t:t + 1, :], (128, 128)).T
        for i in range(kw // 128):
            ls = slice(i * 128, (i + 1) * 128)
            normv[ts, ls] = (hidden[ts, ls].astype(F32) * scale * g[:, ls]).astype(BF16)
        cp = pltpu.make_async_copy(normv.at[ts, :], normed_o.at[ts, :], sem.at[2 + t])
        cp.start()
        copies.append(cp)
    for cp in copies:
        cp.wait()


def per_device(attention_out, residual, trainer_shard, norm_gain):
    tokens, kw = attention_out.shape
    rows, width = trainer_shard.shape
    kh = kw // 2
    hbm = pl.BlockSpec(memory_space=pltpu.HBM)
    vmem = pl.BlockSpec(memory_space=pltpu.VMEM)
    dma = pltpu.SemaphoreType.DMA
    shapes = (
        jax.ShapeDtypeStruct((NX, NX, rows, kw // 2), BF16),
        jax.ShapeDtypeStruct((tokens, kw), BF16),
        jax.ShapeDtypeStruct((tokens, kw), BF16),
    )
    served, hidden, total = pl.pallas_call(
        kernel,
        out_shape=tuple(pltpu.VMEM(a.shape, a.dtype) for a in shapes[:2]) + (pltpu.VMEM((tokens // 128, 128), F32),),
        in_specs=[hbm] * 3,
        out_specs=(vmem,) * 3,
        scratch_shapes=[
            pltpu.VMEM((NX, NX, rows, NR * kh), BF16),
            pltpu.VMEM((rows, NR * kh), BF16),
            pltpu.VMEM((2, NR, tokens, kh), BF16),
            pltpu.VMEM((NR, tokens, 2 * rows), F32),
            pltpu.VMEM((NR, tokens, 2 * rows), BF16),
            pltpu.VMEM((NR, tokens, 2 * rows), BF16),
            pltpu.VMEM((tokens, kw), BF16),
            pltpu.VMEM((tokens, 2 * rows), F32),
            pltpu.VMEM((tokens, 128), F32),
            pltpu.VMEM((NR, tokens // 128, 128), F32),
            dma(()), dma((2, 14)),
            dma(()), dma((3, 2)),
            dma(()), dma((2,)),
            dma(()), dma((5, 3)),
            dma(()), dma((5,)),
            dma(()), dma((2, NR)),
            dma(()), dma(()),
            dma((7,)),
            pltpu.SemaphoreType.REGULAR,
        ],
        compiler_params=pltpu.CompilerParams(
            collective_id=0, has_side_effects=True, vmem_limit_bytes=50 * 1024 * 1024
        ),
        cost_estimate=pl.CostEstimate(
            flops=2 * tokens * kw * width, bytes_accessed=10 * tokens * kw, transcendentals=0
        ),
    )(attention_out, residual, trainer_shard)
    served, hidden, normed = pl.pallas_call(
        finish,
        out_shape=shapes,
        in_specs=[vmem] * 4,
        out_specs=(hbm,) * 3,
        scratch_shapes=[pltpu.VMEM((tokens, kw), BF16), dma((2 + tokens // 128,))],
        compiler_params=pltpu.CompilerParams(vmem_limit_bytes=16 * 1024 * 1024),
        cost_estimate=pl.CostEstimate(
            flops=4 * tokens * kw, bytes_accessed=5 * tokens * kw, transcendentals=tokens
        ),
    )(served, hidden, total, norm_gain)
    return (served.reshape(NX * NX * rows, kw // 2), hidden, normed)


def solution(mesh):
    in_specs = (P("col", "row"), P("col", "row"), P(("row", "col"), None), P("row"))
    out_specs = (P("row", "col"), P("col", "row"), P("col", "row"))
    return jax.shard_map(
        per_device, mesh=mesh, in_specs=in_specs, out_specs=out_specs, check_vma=False
    )
```

```python
import functools

import jax
import jax.numpy as jnp
from jax import lax
from jax.experimental import pallas as pl
from jax.experimental.pallas import tpu as pltpu
from jax.sharding import PartitionSpec as P

MESH = pl.DeviceIdType.MESH
NX = 4
NR = 8
F32 = jnp.float32
BF16 = jnp.bfloat16


def level(v):
    return lax.rem(v + v // 2, 2)


def pair(v):
    return v + 1 - 2 * lax.rem(v, 2)


def mate(v):
    return NX - 1 - v


def kernel(
    att, res, wsh,
    served_o, hidden_o, total_o,
    wbuf, wother, abuf, acc, obuf, ibuf, resv, early, squares, sums,
    c_send, c_recv, p_send, p_recv, n_send, n_recv, y_send, y_recv, s_send, s_recv, o_send, o_recv, q_send, q_recv, l_sem, gate,
):
    rows, kh = wsh.shape[0], abuf.shape[3]
    kw, tokens = 2 * kh, abuf.shape[2]
    part, ht = rows // 2, tokens // 2
    width = NR * kh
    late = 3 * width // 4
    r, c = lax.axis_index("row"), lax.axis_index("col")
    y, core = r // 2, lax.rem(r, 2)
    z, x = c // NX, lax.rem(c, NX)
    px, pz, mx, mz = pair(x), pair(z), mate(x), mate(z)
    colour = lax.rem(level(x) + level(z), 2)
    up, down, across = lax.rem(y + 1, NX), lax.rem(y + NX - 1, NX), lax.rem(y + 2, NX)

    px_dev, pz_dev, diag_dev = (r, z * NX + px), (r, pz * NX + x), (r, pz * NX + px)
    mates = [(r, z * NX + mx), (r, mz * NX + x)]
    ydev = [(up * 2 + core, c), (down * 2 + core, c)]
    sibling = (y * 2 + 1 - core, c)
    peers = [(lax.rem(r + i, NR), c) for i in range(1, NR)]

    barrier = pltpu.get_barrier_semaphore()
    greeted = [px_dev, pz_dev, diag_dev] + mates + peers
    for d in greeted:
        pl.semaphore_signal(barrier, inc=1, device_id=d, device_id_type=MESH)

    def cols(k, col):
        b = lax.rem(col + lax.rem(k, 2) + level(k // 2), 2)
        return pl.ds(pl.multiple_of(k * kw + b * kh, kh), kh)

    def my_cols(col):
        b = lax.rem(col + core + level(y), 2)
        return pl.ds(pl.multiple_of(b * kh, kh), kh)

    def load(src, dst, i):
        pltpu.make_async_copy(src, dst, l_sem.at[i]).start()

    def load_wait(ref, i):
        pltpu.make_async_copy(ref, ref, l_sem.at[i]).wait()

    for p in range(2):
        for k in range(NR):
            ps, ks = pl.ds(p * part, part), pl.ds(k * kh, kh)
            load(wsh.at[ps, cols(k, colour)], wbuf.at[z, x, ps, ks], p)
    for p in range(2):
        for k in range(NR):
            ps, ks = pl.ds(p * part, part), pl.ds(k * kh, kh)
            load(wsh.at[ps, cols(k, 1 - colour)], wother.at[ps, ks], 2 + p)
    load(att.at[:, my_cols(colour)], abuf.at[0, r], 4)
    load(res, resv, 5)
    pl.semaphore_wait(barrier, len(greeted))

    def copy(src, dst, ss, rs, d):
        return pltpu.make_async_remote_copy(
            src_ref=src, dst_ref=dst, send_sem=ss, recv_sem=rs, device_id=d, device_id_type=MESH
        )

    def go(src, dst, ss, rs, d):
        copy(src, dst, ss, rs, d).start()

    def arrived(ref, ss, rs):
        copy(ref, ref, ss, rs, sibling).wait_recv()

    def left(ref, ss, rs):
        copy(ref, ref, ss, rs, sibling).wait_send()

    def source(at_z, at_x, s):
        return (pair(at_z) if s >= 2 else at_z), (pair(at_x) if s % 2 else at_x)

    def w_ref(at_z, at_x, s, p, lo=0, hi=width):
        sz, sx = source(at_z, at_x, s)
        return wbuf.at[sz, sx, pl.ds(p * part, part), pl.ds(lo, hi - lo)]

    def pair_start(s, p):
        ps = pl.ds(p * part, part)
        src = wbuf.at[z, x, ps, :] if s == 3 else wother.at[ps, :]
        d = [px_dev, pz_dev, diag_dev][s - 1]
        go(src, wbuf.at[z, x, ps, :], p_send, p_recv.at[s - 1, p], d)

    def pair_wait(s, p):
        arrived(w_ref(z, x, s, p), p_send, p_recv.at[s - 1, p])

    def mate_start(s, p):
        for l in range(2):
            ref = w_ref(z, x, s, p)
            go(ref, ref, c_send, c_recv.at[max(s - 1, 0)], mates[l])

    def mate_wait(i):
        arrived(wbuf.at[0] if i == 0 else wbuf.at[0, pl.ds(0, 2)], c_send, c_recv.at[i])

    pieces = [(0, 0, width), (1, 0, width), (2, 0, late), (3, 0, late), (2, late, width), (3, late, width)]

    def forward_start(j):
        s, lo, hi = pieces[j]
        ref = w_ref(z, mx, s, 0, lo, hi)
        go(ref, ref, c_send, c_recv.at[3 + j // 2], mates[1])
        ref = w_ref(mz, x, s, 1, lo, hi)
        go(ref, ref, c_send, c_recv.at[3 + j // 2], mates[0])

    def forward_wait(i):
        _, lo, hi = pieces[2 * i]
        arrived(wbuf.at[0, pl.ds(0, 2), :, pl.ds(lo, hi - lo)], c_send, c_recv.at[3 + i])

    t1, t2 = 3 * tokens // 8, 6 * tokens // 8
    groups = [(0, 8 * tokens // 16), (8 * tokens // 16, 8 * tokens // 16)]
    chunks = [(0, 0, t1), (1, *groups[0]), (1, *groups[1]), (0, t1, t2 - t1), (0, t2, tokens - t2)]

    def a_ref(i, at_y, k, lo, n):
        o, t0, _ = chunks[i]
        return abuf.at[o, at_y * 2 + k, pl.ds(t0 + lo, n), :]

    def nbr_ref(g):
        return abuf.at[1, r, pl.ds(*groups[g]), :]

    def nbr_start(g):
        src = att.at[pl.ds(*groups[g]), my_cols(1 - colour)]
        go(src, nbr_ref(g), n_send, n_recv.at[g], pz_dev if g == 0 else px_dev)

    def nbr_wait(g):
        arrived(nbr_ref(g), n_send, n_recv.at[g])

    def y_start(i):
        n = chunks[i][2] // 2
        for piece in range(2):
            for d in range(2):
                ref = a_ref(i, y, core, (piece if d == 0 else 1 - piece) * n, n)
                go(ref, ref, y_send, y_recv.at[i, piece], ydev[d])

    def y_wait(i, piece):
        arrived(a_ref(i, y, core, 0, chunks[i][2]), y_send, y_recv.at[i, piece])

    def y_forward(i):
        n = chunks[i][2] // 2
        for d in range(2):
            ref = a_ref(i, down if d == 0 else up, core, d * n, n)
            go(ref, ref, y_send, y_recv.at[i, 2], ydev[d])

    def y_last(i):
        y_wait(i, 2)

    ys = [y, up, down, across]

    def sib_start(i, j):
        ref = a_ref(i, ys[j], core, 0, chunks[i][2])
        go(ref, ref, s_send, s_recv.at[i], sibling)

    def sib_wait(i):
        o, t0, n = chunks[i]
        arrived(abuf.at[o, pl.ds(0, 4), pl.ds(t0, n), :], s_send, s_recv.at[i])

    nb = 2 * rows

    def blocks(i):
        def pick(*of):
            return jnp.where(i == 0, of[0], jnp.where(i == 1, of[1], jnp.where(i == 2, of[2], of[3])))

        def block(along_z, along_x, second):
            bz, bx = z + along_z * (mz - z), x + along_x * (mx - x)
            return (bz + second * (pair(bz) - bz)) * 2 + bx // 2

        return [
            block(pick(0, 1, 0, 1), pick(0, 0, 1, 1), pick(0, 0, 1, 0)),
            block(pick(0, 0, 1, 1), pick(1, 0, 0, 1), pick(0, 1, 1, 1)),
        ]

    def dot(a, w):
        return lax.dot_general(a, w, (((1,), (1,)), ((), ())), preferred_element_type=F32)

    def product(o, t0, nt, ns, lo=0, hi=width):
        w = [wbuf[n // 2, pl.ds(2 * lax.rem(n, 2), 2), :, lo:hi].reshape(nb, hi - lo) for n in ns]
        a = [abuf[o, k, pl.ds(t0, nt), :] for k in range(lo // kh, hi // kh)]
        return dot(jnp.concatenate(a, axis=1), w[0] if len(w) == 1 else jnp.concatenate(w, axis=0))

    def out_start(g, n, i):
        ts = pl.ds(*groups[g])
        go(obuf.at[n, ts, :], ibuf.at[n, ts, :], o_send, o_recv.at[i], pz_dev if g == 0 else px_dev)

    def out_wait(i):
        arrived(ibuf.at[pl.ds(0, 6), pl.ds(*groups[i]), :] if i < 2 else ibuf.at[0], o_send, o_recv.at[i])

    def nbr_product(g, ns):
        v = product(1, *groups[g], ns).astype(BF16)
        for j, n in enumerate(ns):
            obuf[n, pl.ds(*groups[g]), :] = v[:, j * nb:(j + 1) * nb]
        for n in ns:
            out_start(g, n, g)

    def own_product(t0, nt, ns):
        v = product(0, t0, nt, ns)
        for j, n in enumerate(ns):
            ts = pl.ds(t0, nt)
            at = pl.ds(pl.multiple_of(n * nb, nb), nb)
            acc[n, ts, :] = v[:, j * nb:(j + 1) * nb] + resv[ts, at].astype(F32)

    def finish(n, t0, nt):
        ts = pl.ds(t0, nt)
        hid = (acc[n, ts, :] + ibuf[n, ts, :].astype(F32)).astype(BF16)
        hidden_o[ts, pl.ds(pl.multiple_of(n * nb, nb), nb)] = hid
        wide = hid.astype(F32)
        squares[ts, :] += wide * wide

    zero = r // NR

    def each(lo, hi, f):
        pl.loop(zero + lo, zero + hi)(f)

    for p in range(2):
        load_wait(wbuf.at[z, x, pl.ds(p * part, part), :], p)
        mate_start(0, p)
        if p == 0:
            nbr_start(0)
            load_wait(abuf.at[0, r], 4)
            y_start(0)
    for p in range(2):
        load_wait(wother.at[pl.ds(p * part, part), :], 2 + p)
        pair_start(1, p)
        pair_start(2, p)
    sib_start(0, 0)
    y_wait(0, 0)
    y_forward(0)
    pair_wait(1, 0)
    mate_start(1, 0)
    nbr_start(1)
    y_wait(0, 1)
    sib_start(0, 1)
    sib_start(0, 2)
    pair_wait(1, 1)
    mate_start(1, 1)
    nbr_wait(0)
    y_start(1)
    sib_start(1, 0)
    y_last(0)
    sib_start(0, 3)
    pair_wait(2, 0)
    mate_start(2, 0)
    y_wait(1, 0)
    y_forward(1)
    pair_wait(2, 1)
    pl.semaphore_signal(gate, inc=1, device_id=diag_dev, device_id_type=MESH)
    mate_start(2, 1)
    nbr_wait(1)
    y_start(2)
    sib_start(2, 0)
    y_wait(1, 1)
    sib_start(1, 1)
    sib_start(1, 2)
    pl.semaphore_wait(gate, 1)
    pair_start(3, 0)
    pair_start(3, 1)
    sib_wait(0)
    load_wait(resv, 5)
    mate_wait(0)
    each(0, 1, lambda i: own_product(0, t1, blocks(i)))
    pair_wait(3, 0)
    mate_start(3, 0)
    y_last(1)
    sib_start(1, 3)
    sib_wait(1)
    each(0, 1, lambda i: nbr_product(0, blocks(i)))
    pair_wait(3, 1)
    mate_start(3, 1)
    forward_start(0)
    forward_start(1)
    y_wait(2, 0)
    y_forward(2)
    y_start(3)
    sib_start(3, 0)
    each(1, 2, lambda i: nbr_product(0, blocks(i)))
    each(1, 2, lambda i: own_product(0, t1, blocks(i)))
    mate_wait(1)
    forward_start(2)
    y_wait(2, 1)
    sib_start(2, 1)
    sib_start(2, 2)
    mate_wait(2)
    for j in range(3, 6):
        forward_start(j)
    each(2, 3, lambda i: nbr_product(0, blocks(i)))
    y_last(2)
    sib_start(2, 3)
    sib_wait(2)
    each(0, 2, lambda i: nbr_product(1, blocks(i)))
    y_wait(3, 0)
    y_forward(3)
    y_start(4)
    sib_start(4, 0)
    each(2, 3, lambda i: nbr_product(1, blocks(i)))
    each(2, 3, lambda i: own_product(0, t1, blocks(i)))
    y_wait(3, 1)
    sib_start(3, 1)
    sib_start(3, 2)
    squares[...] = jnp.zeros_like(squares)

    out_wait(0)

    @pl.loop(0, 3)
    def _(i):
        for n in blocks(i):
            finish(n, 0, t1)

    forward_wait(0)
    first, last = blocks(3)

    @pl.loop(0, 2)
    def _(h):
        ts = pl.ds(pl.multiple_of(h * ht, ht), ht)
        obuf[first, ts, :] = product(1, ts.start, ht, [first]).astype(BF16)

    out_start(0, first, 3)
    out_start(1, first, 2)
    y_last(3)
    sib_start(3, 3)
    sib_wait(3)
    each(0, 1, lambda i: own_product(t1, t2 - t1, blocks(i)))
    y_wait(4, 0)
    y_forward(4)
    each(1, 3, lambda i: own_product(t1, t2 - t1, blocks(i)))
    forward_wait(1)

    @pl.loop(0, 2)
    def _(h):
        ts = pl.ds(pl.multiple_of(h * ht, ht), ht)
        early[ts, :] = product(1, ts.start, ht, [last], 0, late)

    y_wait(4, 1)
    sib_start(4, 1)
    sib_start(4, 2)
    forward_wait(2)

    @pl.loop(0, 2)
    def _(i):
        ts = pl.ds(pl.multiple_of((1 - i) * ht, ht), ht)
        obuf[last, ts, :] = (early[ts, :] + product(1, ts.start, ht, [last], late, width)).astype(BF16)

        @pl.when(i == 0)
        def _():
            out_start(1, last, 3)

        @pl.when(i == 1)
        def _():
            out_start(0, last, 2)

    y_last(4)
    sib_start(4, 3)
    out_wait(1)

    @pl.loop(0, 2)
    def _(i):
        own_product(pl.multiple_of(i * t1, t1), t1, [first, last])
        for j in range(3):
            k = 3 * i + j
            one, other = blocks(k // 2)
            n = jnp.where(lax.rem(k, 2) == 0, one, other)
            finish(n, t1, t2 - t1)

    sib_wait(4)
    pl.loop(0, 2)(lambda i: own_product(t2, tokens - t2, blocks(2 * i) + blocks(2 * i + 1)))

    served = pltpu.make_async_copy(
        wbuf.at[:, :, :, pl.ds(pl.multiple_of((c // 2) * kh, kh), kh)], served_o, l_sem.at[6])
    served.start()

    @pl.loop(0, 3)
    def _(i):
        for n in blocks(i):
            finish(n, t2, tokens - t2)

    for i, n in ((2, first), (3, last)):
        out_wait(i)
        finish(n, 0, tokens)

    for t in range(tokens // 128):
        sums[r, t:t + 1, :] = jnp.sum(squares[t * 128:(t + 1) * 128, :].T, axis=0, keepdims=True)
    for i in (3, 4, 2, 5, 1, 6, 0):
        go(sums.at[r], sums.at[r], q_send, q_recv, peers[i])
    served.wait()
    left(wbuf.at[pl.ds(0, 3)], c_send, c_recv.at[0])
    left(wbuf.at[0, pl.ds(0, 3)], p_send, p_recv.at[0, 0])
    left(abuf.at[0, 0], n_send, n_recv.at[0])
    left(abuf.at[0, pl.ds(0, 6)], y_send, y_recv.at[0, 0])
    left(abuf.at[0], s_send, s_recv.at[0])
    left(obuf, o_send, o_recv.at[0])
    arrived(sums.at[pl.ds(0, NR - 1)], q_send, q_recv)
    total = sums[0]
    for i in range(1, NR):
        total = total + sums[i]
    total_o[...] = total
    left(sums.at[pl.ds(0, NR - 1)], q_send, q_recv)


def finish(served, hidden, total, gain, served_o, hidden_o, normed_o, normv, sem):
    tokens, kw = hidden.shape
    copies = [
        pltpu.make_async_copy(hidden, hidden_o, sem.at[0]),
        pltpu.make_async_copy(served, served_o, sem.at[1]),
    ]
    for cp in copies:
        cp.start()
    inv = lax.rsqrt(total[...] / (NR * kw) + 1e-05)
    g = gain[...].astype(F32)[None, :]
    for t in range(tokens // 128):
        ts = slice(t * 128, (t + 1) * 128)
        scale = jnp.broadcast_to(inv[t:t + 1, :], (128, 128)).T
        for i in range(kw // 128):
            ls = slice(i * 128, (i + 1) * 128)
            normv[ts, ls] = (hidden[ts, ls].astype(F32) * scale * g[:, ls]).astype(BF16)
        cp = pltpu.make_async_copy(normv.at[ts, :], normed_o.at[ts, :], sem.at[2 + t])
        cp.start()
        copies.append(cp)
    for cp in copies:
        cp.wait()


def per_device(attention_out, residual, trainer_shard, norm_gain):
    tokens, kw = attention_out.shape
    rows, width = trainer_shard.shape
    kh = kw // 2
    hbm = pl.BlockSpec(memory_space=pltpu.HBM)
    vmem = pl.BlockSpec(memory_space=pltpu.VMEM)
    dma = pltpu.SemaphoreType.DMA
    shapes = (
        jax.ShapeDtypeStruct((NX, NX, rows, kw // 2), BF16),
        jax.ShapeDtypeStruct((tokens, kw), BF16),
        jax.ShapeDtypeStruct((tokens, kw), BF16),
    )
    served, hidden, total = pl.pallas_call(
        kernel,
        out_shape=tuple(pltpu.VMEM(a.shape, a.dtype) for a in shapes[:2]) + (pltpu.VMEM((tokens // 128, 128), F32),),
        in_specs=[hbm] * 3,
        out_specs=(vmem,) * 3,
        scratch_shapes=[
            pltpu.VMEM((NX, NX, rows, NR * kh), BF16),
            pltpu.VMEM((rows, NR * kh), BF16),
            pltpu.VMEM((2, NR, tokens, kh), BF16),
            pltpu.VMEM((NR, tokens, 2 * rows), F32),
            pltpu.VMEM((NR, tokens, 2 * rows), BF16),
            pltpu.VMEM((NR, tokens, 2 * rows), BF16),
            pltpu.VMEM((tokens, kw), BF16),
            pltpu.VMEM((tokens, 2 * rows), F32),
            pltpu.VMEM((tokens, 128), F32),
            pltpu.VMEM((NR, tokens // 128, 128), F32),
            dma(()), dma((6,)),
            dma(()), dma((3, 2)),
            dma(()), dma((2,)),
            dma(()), dma((5, 3)),
            dma(()), dma((5,)),
            dma(()), dma((4,)),
            dma(()), dma(()),
            dma((7,)),
            pltpu.SemaphoreType.REGULAR,
        ],
        compiler_params=pltpu.CompilerParams(
            collective_id=0, has_side_effects=True, vmem_limit_bytes=50 * 1024 * 1024
        ),
        cost_estimate=pl.CostEstimate(
            flops=2 * tokens * kw * width, bytes_accessed=10 * tokens * kw, transcendentals=0
        ),
    )(attention_out, residual, trainer_shard)
    served, hidden, normed = pl.pallas_call(
        finish,
        out_shape=shapes,
        in_specs=[vmem] * 4,
        out_specs=(hbm,) * 3,
        scratch_shapes=[pltpu.VMEM((tokens, kw), BF16), dma((2 + tokens // 128,))],
        compiler_params=pltpu.CompilerParams(vmem_limit_bytes=16 * 1024 * 1024),
        cost_estimate=pl.CostEstimate(
            flops=4 * tokens * kw, bytes_accessed=5 * tokens * kw, transcendentals=tokens
        ),
    )(served, hidden, total, norm_gain)
    return (served.reshape(NX * NX * rows, kw // 2), hidden, normed)


def solution(mesh):
    in_specs = (P("col", "row"), P("col", "row"), P(("row", "col"), None), P("row"))
    out_specs = (P("row", "col"), P("col", "row"), P("col", "row"))
    return jax.shard_map(
        per_device, mesh=mesh, in_specs=in_specs, out_specs=out_specs, check_vma=False
    )
```

```python
import functools

import jax
import jax.numpy as jnp
from jax import lax
from jax.experimental import pallas as pl
from jax.experimental.pallas import tpu as pltpu
from jax.sharding import PartitionSpec as P

MESH = pl.DeviceIdType.MESH
NX = 4
NR = 8
F32 = jnp.float32
BF16 = jnp.bfloat16


def level(v):
    return lax.rem(v + v // 2, 2)


def pair(v):
    return v + 1 - 2 * lax.rem(v, 2)


def mate(v):
    return NX - 1 - v


def kernel(
    att, res, wsh,
    served_o, hidden_o, total_o,
    wbuf, wother, abuf, acc, obuf, ibuf, resv, early, squares, sums,
    c_send, c_recv, p_send, p_recv, n_send, n_recv, y_send, y_recv, s_send, s_recv, o_send, o_recv, q_send, q_recv, l_sem, gate,
):
    rows, kh = wsh.shape[0], abuf.shape[3]
    kw, tokens = 2 * kh, abuf.shape[2]
    part, ht = rows // 2, tokens // 2
    width = NR * kh
    late = 3 * width // 4
    r, c = lax.axis_index("row"), lax.axis_index("col")
    y, core = r // 2, lax.rem(r, 2)
    z, x = c // NX, lax.rem(c, NX)
    px, pz, mx, mz = pair(x), pair(z), mate(x), mate(z)
    colour = lax.rem(level(x) + level(z), 2)
    up, down, across = lax.rem(y + 1, NX), lax.rem(y + NX - 1, NX), lax.rem(y + 2, NX)

    px_dev, pz_dev, diag_dev = (r, z * NX + px), (r, pz * NX + x), (r, pz * NX + px)
    mates = [(r, z * NX + mx), (r, mz * NX + x)]
    ydev = [(up * 2 + core, c), (down * 2 + core, c)]
    sibling = (y * 2 + 1 - core, c)
    peers = [(lax.rem(r + i, NR), c) for i in range(1, NR)]

    barrier = pltpu.get_barrier_semaphore()
    greeted = [px_dev, pz_dev, diag_dev] + mates + peers
    for d in greeted:
        pl.semaphore_signal(barrier, inc=1, device_id=d, device_id_type=MESH)

    def cols(k, col):
        b = lax.rem(col + lax.rem(k, 2) + level(k // 2), 2)
        return pl.ds(pl.multiple_of(k * kw + b * kh, kh), kh)

    def my_cols(col):
        b = lax.rem(col + core + level(y), 2)
        return pl.ds(pl.multiple_of(b * kh, kh), kh)

    def load(src, dst, i):
        pltpu.make_async_copy(src, dst, l_sem.at[i]).start()

    def load_wait(ref, i):
        pltpu.make_async_copy(ref, ref, l_sem.at[i]).wait()

    for p in range(2):
        for k in range(NR):
            ps, ks = pl.ds(p * part, part), pl.ds(k * kh, kh)
            load(wsh.at[ps, cols(k, colour)], wbuf.at[z, x, ps, ks], p)
    for p in range(2):
        for k in range(NR):
            ps, ks = pl.ds(p * part, part), pl.ds(k * kh, kh)
            load(wsh.at[ps, cols(k, 1 - colour)], wother.at[ps, ks], 2 + p)
    load(att.at[:, my_cols(colour)], abuf.at[0, r], 4)
    load(res, resv, 5)
    pl.semaphore_wait(barrier, len(greeted))

    def copy(src, dst, ss, rs, d):
        return pltpu.make_async_remote_copy(
            src_ref=src, dst_ref=dst, send_sem=ss, recv_sem=rs, device_id=d, device_id_type=MESH
        )

    def go(src, dst, ss, rs, d):
        copy(src, dst, ss, rs, d).start()

    def arrived(ref, ss, rs):
        copy(ref, ref, ss, rs, sibling).wait_recv()

    def left(ref, ss, rs):
        copy(ref, ref, ss, rs, sibling).wait_send()

    def source(at_z, at_x, s):
        return (pair(at_z) if s >= 2 else at_z), (pair(at_x) if s % 2 else at_x)

    def w_ref(at_z, at_x, s, p, lo=0, hi=width):
        sz, sx = source(at_z, at_x, s)
        return wbuf.at[sz, sx, pl.ds(p * part, part), pl.ds(lo, hi - lo)]

    def pair_start(s, p):
        ps = pl.ds(p * part, part)
        src = wbuf.at[z, x, ps, :] if s == 3 else wother.at[ps, :]
        d = [px_dev, pz_dev, diag_dev][s - 1]
        go(src, wbuf.at[z, x, ps, :], p_send, p_recv.at[s - 1, p], d)

    def pair_wait(s, p):
        arrived(w_ref(z, x, s, p), p_send, p_recv.at[s - 1, p])

    def mate_start(s, p):
        for l in range(2):
            ref = w_ref(z, x, s, p)
            go(ref, ref, c_send, c_recv.at[max(s - 1, 0)], mates[l])

    def mate_wait(i):
        arrived(wbuf.at[0] if i == 0 else wbuf.at[0, pl.ds(0, 2)], c_send, c_recv.at[i])

    pieces = [(0, 0, width), (1, 0, width), (2, 0, late), (3, 0, late), (2, late, width), (3, late, width)]

    def forward_start(j):
        s, lo, hi = pieces[j]
        ref = w_ref(z, mx, s, 0, lo, hi)
        go(ref, ref, c_send, c_recv.at[3 + j // 2], mates[1])
        ref = w_ref(mz, x, s, 1, lo, hi)
        go(ref, ref, c_send, c_recv.at[3 + j // 2], mates[0])

    def forward_wait(i):
        _, lo, hi = pieces[2 * i]
        arrived(wbuf.at[0, pl.ds(0, 2), :, pl.ds(lo, hi - lo)], c_send, c_recv.at[3 + i])

    t1, t2 = 3 * tokens // 8, 6 * tokens // 8
    groups = [(0, 8 * tokens // 16), (8 * tokens // 16, 8 * tokens // 16)]
    chunks = [(0, 0, t1), (1, *groups[0]), (1, *groups[1]), (0, t1, t2 - t1), (0, t2, tokens - t2)]

    def a_ref(i, at_y, k, lo, n):
        o, t0, _ = chunks[i]
        return abuf.at[o, at_y * 2 + k, pl.ds(t0 + lo, n), :]

    def nbr_ref(g):
        return abuf.at[1, r, pl.ds(*groups[g]), :]

    def nbr_start(g):
        src = att.at[pl.ds(*groups[g]), my_cols(1 - colour)]
        go(src, nbr_ref(g), n_send, n_recv.at[g], pz_dev if g == 0 else px_dev)

    def nbr_wait(g):
        arrived(nbr_ref(g), n_send, n_recv.at[g])

    def y_start(i):
        n = chunks[i][2] // 2
        for piece in range(2):
            for d in range(2):
                ref = a_ref(i, y, core, (piece if d == 0 else 1 - piece) * n, n)
                go(ref, ref, y_send, y_recv.at[i, piece], ydev[d])

    def y_wait(i, piece):
        arrived(a_ref(i, y, core, 0, chunks[i][2]), y_send, y_recv.at[i, piece])

    def y_forward(i):
        n = chunks[i][2] // 2
        for d in range(2):
            ref = a_ref(i, down if d == 0 else up, core, d * n, n)
            go(ref, ref, y_send, y_recv.at[i, 2], ydev[d])

    def y_last(i):
        y_wait(i, 2)

    ys = [y, up, down, across]

    def sib_start(i, j):
        ref = a_ref(i, ys[j], core, 0, chunks[i][2])
        go(ref, ref, s_send, s_recv.at[i], sibling)

    def sib_wait(i):
        o, t0, n = chunks[i]
        arrived(abuf.at[o, pl.ds(0, 4), pl.ds(t0, n), :], s_send, s_recv.at[i])

    nb = 2 * rows

    def blocks(i):
        def pick(*of):
            return jnp.where(i == 0, of[0], jnp.where(i == 1, of[1], jnp.where(i == 2, of[2], of[3])))

        def block(along_z, along_x, second):
            bz, bx = z + along_z * (mz - z), x + along_x * (mx - x)
            return (bz + second * (pair(bz) - bz)) * 2 + bx // 2

        return [
            block(pick(0, 1, 0, 1), pick(0, 0, 1, 1), pick(0, 0, 1, 0)),
            block(pick(0, 0, 1, 1), pick(1, 0, 0, 1), pick(0, 1, 1, 1)),
        ]

    def dot(a, w):
        return lax.dot_general(a, w, (((1,), (1,)), ((), ())), preferred_element_type=F32)

    def product(o, t0, nt, ns, lo=0, hi=width):
        w = [wbuf[n // 2, pl.ds(2 * lax.rem(n, 2), 2), :, lo:hi].reshape(nb, hi - lo) for n in ns]
        a = [abuf[o, k, pl.ds(t0, nt), :] for k in range(lo // kh, hi // kh)]
        return dot(jnp.concatenate(a, axis=1), w[0] if len(w) == 1 else jnp.concatenate(w, axis=0))

    def out_start(g, n, i):
        ts = pl.ds(*groups[g])
        go(obuf.at[n, ts, :], ibuf.at[n, ts, :], o_send, o_recv.at[i], pz_dev if g == 0 else px_dev)

    def out_wait(i):
        arrived(ibuf.at[pl.ds(0, 6), pl.ds(*groups[i]), :] if i < 2 else ibuf.at[0], o_send, o_recv.at[i])

    def nbr_product(g, ns):
        v = product(1, *groups[g], ns).astype(BF16)
        for j, n in enumerate(ns):
            obuf[n, pl.ds(*groups[g]), :] = v[:, j * nb:(j + 1) * nb]
        for n in ns:
            out_start(g, n, g)

    def own_product(t0, nt, ns):
        v = product(0, t0, nt, ns)
        for j, n in enumerate(ns):
            ts = pl.ds(t0, nt)
            at = pl.ds(pl.multiple_of(n * nb, nb), nb)
            acc[n, ts, :] = v[:, j * nb:(j + 1) * nb] + resv[ts, at].astype(F32)

    def finish(n, t0, nt):
        ts = pl.ds(t0, nt)
        hid = (acc[n, ts, :] + ibuf[n, ts, :].astype(F32)).astype(BF16)
        hidden_o[ts, pl.ds(pl.multiple_of(n * nb, nb), nb)] = hid
        wide = hid.astype(F32)
        squares[ts, :] += wide * wide

    zero = r // NR

    def each(lo, hi, f):
        pl.loop(zero + lo, zero + hi)(f)

    for p in range(2):
        load_wait(wbuf.at[z, x, pl.ds(p * part, part), :], p)
        mate_start(0, p)
        if p == 0:
            nbr_start(0)
            load_wait(abuf.at[0, r], 4)
            y_start(0)
    for p in range(2):
        load_wait(wother.at[pl.ds(p * part, part), :], 2 + p)
        pair_start(1, p)
        pair_start(2, p)
    sib_start(0, 0)
    y_wait(0, 0)
    y_forward(0)
    pair_wait(1, 0)
    mate_start(1, 0)
    nbr_start(1)
    y_wait(0, 1)
    sib_start(0, 1)
    sib_start(0, 2)
    pair_wait(1, 1)
    mate_start(1, 1)
    nbr_wait(0)
    y_start(1)
    sib_start(1, 0)
    y_last(0)
    sib_start(0, 3)
    pair_wait(2, 0)
    mate_start(2, 0)
    y_wait(1, 0)
    y_forward(1)
    pair_wait(2, 1)
    pl.semaphore_signal(gate, inc=1, device_id=diag_dev, device_id_type=MESH)
    mate_start(2, 1)
    nbr_wait(1)
    y_start(2)
    sib_start(2, 0)
    y_wait(1, 1)
    sib_start(1, 1)
    sib_start(1, 2)
    pl.semaphore_wait(gate, 1)
    pair_start(3, 0)
    pair_start(3, 1)
    sib_wait(0)
    load_wait(resv, 5)
    mate_wait(0)
    each(0, 1, lambda i: own_product(0, t1, blocks(i)))
    pair_wait(3, 0)
    mate_start(3, 0)
    y_last(1)
    sib_start(1, 3)
    sib_wait(1)
    each(0, 1, lambda i: nbr_product(0, blocks(i)))
    pair_wait(3, 1)
    mate_start(3, 1)
    forward_start(0)
    forward_start(1)
    y_wait(2, 0)
    y_forward(2)
    y_start(3)
    sib_start(3, 0)
    each(1, 2, lambda i: nbr_product(0, blocks(i)))
    each(1, 2, lambda i: own_product(0, t1, blocks(i)))
    mate_wait(1)
    forward_start(2)
    y_wait(2, 1)
    sib_start(2, 1)
    sib_start(2, 2)
    mate_wait(2)
    for j in range(3, 6):
        forward_start(j)
    each(2, 3, lambda i: nbr_product(0, blocks(i)))
    y_last(2)
    sib_start(2, 3)
    sib_wait(2)
    each(0, 2, lambda i: nbr_product(1, blocks(i)))
    y_wait(3, 0)
    y_forward(3)
    y_start(4)
    sib_start(4, 0)
    each(2, 3, lambda i: nbr_product(1, blocks(i)))
    each(2, 3, lambda i: own_product(0, t1, blocks(i)))
    y_wait(3, 1)
    sib_start(3, 1)
    sib_start(3, 2)
    squares[...] = jnp.zeros_like(squares)

    out_wait(0)

    @pl.loop(0, 3)
    def _(i):
        for n in blocks(i):
            finish(n, 0, t1)

    forward_wait(0)
    first, last = blocks(3)

    @pl.loop(0, 2)
    def _(h):
        ts = pl.ds(pl.multiple_of(h * ht, ht), ht)
        obuf[first, ts, :] = product(1, ts.start, ht, [first]).astype(BF16)

    out_start(0, first, 3)
    out_start(1, first, 2)
    y_last(3)
    sib_start(3, 3)
    sib_wait(3)
    each(0, 1, lambda i: own_product(t1, t2 - t1, blocks(i)))
    y_wait(4, 0)
    y_forward(4)
    each(1, 3, lambda i: own_product(t1, t2 - t1, blocks(i)))
    forward_wait(1)

    @pl.loop(0, 2)
    def _(h):
        ts = pl.ds(pl.multiple_of(h * ht, ht), ht)
        early[ts, :] = product(1, ts.start, ht, [last], 0, late)

    y_wait(4, 1)
    sib_start(4, 1)
    sib_start(4, 2)
    forward_wait(2)

    @pl.loop(0, 2)
    def _(i):
        ts = pl.ds(pl.multiple_of((1 - i) * ht, ht), ht)
        obuf[last, ts, :] = (early[ts, :] + product(1, ts.start, ht, [last], late, width)).astype(BF16)

        @pl.when(i == 0)
        def _():
            out_start(1, last, 3)

        @pl.when(i == 1)
        def _():
            out_start(0, last, 2)

    y_last(4)
    sib_start(4, 3)
    pl.loop(0, 2)(lambda i: own_product(pl.multiple_of(i * t1, t1), t1, [first, last]))
    sib_wait(4)
    out_wait(1)

    @pl.loop(0, 2)
    def _(i):
        own_product(t2, tokens - t2, blocks(2 * i) + blocks(2 * i + 1))
        for j in range(3):
            k = 3 * i + j
            one, other = blocks(k // 2)
            finish(jnp.where(lax.rem(k, 2) == 0, one, other), t1, t2 - t1)

    served = pltpu.make_async_copy(
        wbuf.at[:, :, :, pl.ds(pl.multiple_of((c // 2) * kh, kh), kh)], served_o, l_sem.at[6])
    served.start()

    @pl.loop(0, 3)
    def _(i):
        for n in blocks(i):
            finish(n, t2, tokens - t2)

    for i, n in ((2, first), (3, last)):
        out_wait(i)
        finish(n, 0, tokens)

    for t in range(tokens // 128):
        sums[r, t:t + 1, :] = jnp.sum(squares[t * 128:(t + 1) * 128, :].T, axis=0, keepdims=True)
    for i in (3, 4, 2, 5, 1, 6, 0):
        go(sums.at[r], sums.at[r], q_send, q_recv, peers[i])
    served.wait()
    left(wbuf.at[pl.ds(0, 3)], c_send, c_recv.at[0])
    left(wbuf.at[0, pl.ds(0, 3)], p_send, p_recv.at[0, 0])
    left(abuf.at[0, 0], n_send, n_recv.at[0])
    left(abuf.at[0, pl.ds(0, 6)], y_send, y_recv.at[0, 0])
    left(abuf.at[0], s_send, s_recv.at[0])
    left(obuf, o_send, o_recv.at[0])
    arrived(sums.at[pl.ds(0, NR - 1)], q_send, q_recv)
    total = sums[0]
    for i in range(1, NR):
        total = total + sums[i]
    total_o[...] = total
    left(sums.at[pl.ds(0, NR - 1)], q_send, q_recv)


def finish(served, hidden, total, gain, served_o, hidden_o, normed_o, normv, sem):
    tokens, kw = hidden.shape
    copies = [
        pltpu.make_async_copy(hidden, hidden_o, sem.at[0]),
        pltpu.make_async_copy(served, served_o, sem.at[1]),
    ]
    for cp in copies:
        cp.start()
    inv = lax.rsqrt(total[...] / (NR * kw) + 1e-05)
    g = gain[...].astype(F32)[None, :]
    for t in range(tokens // 128):
        ts = slice(t * 128, (t + 1) * 128)
        scale = jnp.broadcast_to(inv[t:t + 1, :], (128, 128)).T
        for i in range(kw // 128):
            ls = slice(i * 128, (i + 1) * 128)
            normv[ts, ls] = (hidden[ts, ls].astype(F32) * scale * g[:, ls]).astype(BF16)
        cp = pltpu.make_async_copy(normv.at[ts, :], normed_o.at[ts, :], sem.at[2 + t])
        cp.start()
        copies.append(cp)
    for cp in copies:
        cp.wait()


def per_device(attention_out, residual, trainer_shard, norm_gain):
    tokens, kw = attention_out.shape
    rows, width = trainer_shard.shape
    kh = kw // 2
    hbm = pl.BlockSpec(memory_space=pltpu.HBM)
    vmem = pl.BlockSpec(memory_space=pltpu.VMEM)
    dma = pltpu.SemaphoreType.DMA
    shapes = (
        jax.ShapeDtypeStruct((NX, NX, rows, kw // 2), BF16),
        jax.ShapeDtypeStruct((tokens, kw), BF16),
        jax.ShapeDtypeStruct((tokens, kw), BF16),
    )
    served, hidden, total = pl.pallas_call(
        kernel,
        out_shape=tuple(pltpu.VMEM(a.shape, a.dtype) for a in shapes[:2]) + (pltpu.VMEM((tokens // 128, 128), F32),),
        in_specs=[hbm] * 3,
        out_specs=(vmem,) * 3,
        scratch_shapes=[
            pltpu.VMEM((NX, NX, rows, NR * kh), BF16),
            pltpu.VMEM((rows, NR * kh), BF16),
            pltpu.VMEM((2, NR, tokens, kh), BF16),
            pltpu.VMEM((NR, tokens, 2 * rows), F32),
            pltpu.VMEM((NR, tokens, 2 * rows), BF16),
            pltpu.VMEM((NR, tokens, 2 * rows), BF16),
            pltpu.VMEM((tokens, kw), BF16),
            pltpu.VMEM((tokens, 2 * rows), F32),
            pltpu.VMEM((tokens, 128), F32),
            pltpu.VMEM((NR, tokens // 128, 128), F32),
            dma(()), dma((6,)),
            dma(()), dma((3, 2)),
            dma(()), dma((2,)),
            dma(()), dma((5, 3)),
            dma(()), dma((5,)),
            dma(()), dma((4,)),
            dma(()), dma(()),
            dma((7,)),
            pltpu.SemaphoreType.REGULAR,
        ],
        compiler_params=pltpu.CompilerParams(
            collective_id=0, has_side_effects=True, vmem_limit_bytes=50 * 1024 * 1024
        ),
        cost_estimate=pl.CostEstimate(
            flops=2 * tokens * kw * width, bytes_accessed=10 * tokens * kw, transcendentals=0
        ),
    )(attention_out, residual, trainer_shard)
    served, hidden, normed = pl.pallas_call(
        finish,
        out_shape=shapes,
        in_specs=[vmem] * 4,
        out_specs=(hbm,) * 3,
        scratch_shapes=[pltpu.VMEM((tokens, kw), BF16), dma((2 + tokens // 128,))],
        compiler_params=pltpu.CompilerParams(vmem_limit_bytes=16 * 1024 * 1024),
        cost_estimate=pl.CostEstimate(
            flops=4 * tokens * kw, bytes_accessed=5 * tokens * kw, transcendentals=tokens
        ),
    )(served, hidden, total, norm_gain)
    return (served.reshape(NX * NX * rows, kw // 2), hidden, normed)


def solution(mesh):
    in_specs = (P("col", "row"), P("col", "row"), P(("row", "col"), None), P("row"))
    out_specs = (P("row", "col"), P("col", "row"), P("col", "row"))
    return jax.shard_map(
        per_device, mesh=mesh, in_specs=in_specs, out_specs=out_specs, check_vma=False
    )
```

```python
import functools

import jax
import jax.numpy as jnp
from jax import lax
from jax.experimental import pallas as pl
from jax.experimental.pallas import tpu as pltpu
from jax.sharding import PartitionSpec as P

MESH = pl.DeviceIdType.MESH
NX = 4
NR = 8
F32 = jnp.float32
BF16 = jnp.bfloat16


def level(v):
    return lax.rem(v + v // 2, 2)


def pair(v):
    return v + 1 - 2 * lax.rem(v, 2)


def mate(v):
    return NX - 1 - v


def kernel(
    att, res, wsh,
    served_o, hidden_o, total_o,
    wbuf, wother, abuf, acc, obuf, ibuf, resv, early, squares, sums,
    c_send, c_recv, p_send, p_recv, n_send, n_recv, y_send, y_recv, s_send, s_recv, o_send, o_recv, q_send, q_recv, l_sem, gate,
):
    rows, kh = wsh.shape[0], abuf.shape[3]
    kw, tokens = 2 * kh, abuf.shape[2]
    part, ht = rows // 2, tokens // 2
    width = NR * kh
    late = 3 * width // 4
    r, c = lax.axis_index("row"), lax.axis_index("col")
    y, core = r // 2, lax.rem(r, 2)
    z, x = c // NX, lax.rem(c, NX)
    px, pz, mx, mz = pair(x), pair(z), mate(x), mate(z)
    colour = lax.rem(level(x) + level(z), 2)
    up, down, across = lax.rem(y + 1, NX), lax.rem(y + NX - 1, NX), lax.rem(y + 2, NX)

    px_dev, pz_dev, diag_dev = (r, z * NX + px), (r, pz * NX + x), (r, pz * NX + px)
    mates = [(r, z * NX + mx), (r, mz * NX + x)]
    ydev = [(up * 2 + core, c), (down * 2 + core, c)]
    sibling = (y * 2 + 1 - core, c)
    peers = [(lax.rem(r + i, NR), c) for i in range(1, NR)]

    barrier = pltpu.get_barrier_semaphore()
    greeted = [px_dev, pz_dev, diag_dev] + mates + peers
    for d in greeted:
        pl.semaphore_signal(barrier, inc=1, device_id=d, device_id_type=MESH)

    def cols(k, col):
        b = lax.rem(col + lax.rem(k, 2) + level(k // 2), 2)
        return pl.ds(pl.multiple_of(k * kw + b * kh, kh), kh)

    def my_cols(col):
        b = lax.rem(col + core + level(y), 2)
        return pl.ds(pl.multiple_of(b * kh, kh), kh)

    def load(src, dst, i):
        pltpu.make_async_copy(src, dst, l_sem.at[i]).start()

    def load_wait(ref, i):
        pltpu.make_async_copy(ref, ref, l_sem.at[i]).wait()

    for p in range(2):
        for k in range(NR):
            ps, ks = pl.ds(p * part, part), pl.ds(k * kh, kh)
            load(wsh.at[ps, cols(k, colour)], wbuf.at[z, x, ps, ks], p)
    for p in range(2):
        for k in range(NR):
            ps, ks = pl.ds(p * part, part), pl.ds(k * kh, kh)
            load(wsh.at[ps, cols(k, 1 - colour)], wother.at[ps, ks], 2 + p)
    load(att.at[:, my_cols(colour)], abuf.at[0, r], 4)
    load(res, resv, 5)
    pl.semaphore_wait(barrier, len(greeted))

    def copy(src, dst, ss, rs, d):
        return pltpu.make_async_remote_copy(
            src_ref=src, dst_ref=dst, send_sem=ss, recv_sem=rs, device_id=d, device_id_type=MESH
        )

    def go(src, dst, ss, rs, d):
        copy(src, dst, ss, rs, d).start()

    def arrived(ref, ss, rs):
        copy(ref, ref, ss, rs, sibling).wait_recv()

    def left(ref, ss, rs):
        copy(ref, ref, ss, rs, sibling).wait_send()

    def source(at_z, at_x, s):
        return (pair(at_z) if s >= 2 else at_z), (pair(at_x) if s % 2 else at_x)

    def w_ref(at_z, at_x, s, p, lo=0, hi=width):
        sz, sx = source(at_z, at_x, s)
        return wbuf.at[sz, sx, pl.ds(p * part, part), pl.ds(lo, hi - lo)]

    def pair_start(s, p):
        ps = pl.ds(p * part, part)
        src = wbuf.at[z, x, ps, :] if s == 3 else wother.at[ps, :]
        d = [px_dev, pz_dev, diag_dev][s - 1]
        go(src, wbuf.at[z, x, ps, :], p_send, p_recv.at[s - 1, p], d)

    def pair_wait(s, p):
        arrived(w_ref(z, x, s, p), p_send, p_recv.at[s - 1, p])

    def mate_start(s, p):
        for l in range(2):
            ref = w_ref(z, x, s, p)
            go(ref, ref, c_send, c_recv.at[max(s - 1, 0)], mates[l])

    def mate_wait(i):
        arrived(wbuf.at[0] if i == 0 else wbuf.at[0, pl.ds(0, 2)], c_send, c_recv.at[i])

    pieces = [(0, 0, width), (1, 0, width), (2, 0, late), (3, 0, late), (2, late, width), (3, late, width)]

    def forward_start(j):
        s, lo, hi = pieces[j]
        ref = w_ref(z, mx, s, 0, lo, hi)
        go(ref, ref, c_send, c_recv.at[3 + j // 2], mates[1])
        ref = w_ref(mz, x, s, 1, lo, hi)
        go(ref, ref, c_send, c_recv.at[3 + j // 2], mates[0])

    def forward_wait(i):
        _, lo, hi = pieces[2 * i]
        arrived(wbuf.at[0, pl.ds(0, 2), :, pl.ds(lo, hi - lo)], c_send, c_recv.at[3 + i])

    t1, t2 = 3 * tokens // 8, 13 * tokens // 16
    groups = [(0, 8 * tokens // 16), (8 * tokens // 16, 8 * tokens // 16)]
    chunks = [(0, 0, t1), (1, *groups[0]), (1, *groups[1]), (0, t1, t2 - t1), (0, t2, tokens - t2)]

    def a_ref(i, at_y, k, lo, n):
        o, t0, _ = chunks[i]
        return abuf.at[o, at_y * 2 + k, pl.ds(t0 + lo, n), :]

    def nbr_ref(g):
        return abuf.at[1, r, pl.ds(*groups[g]), :]

    def nbr_start(g):
        src = att.at[pl.ds(*groups[g]), my_cols(1 - colour)]
        go(src, nbr_ref(g), n_send, n_recv.at[g], pz_dev if g == 0 else px_dev)

    def nbr_wait(g):
        arrived(nbr_ref(g), n_send, n_recv.at[g])

    def y_start(i):
        n = chunks[i][2] // 2
        for piece in range(2):
            for d in range(2):
                ref = a_ref(i, y, core, (piece if d == 0 else 1 - piece) * n, n)
                go(ref, ref, y_send, y_recv.at[i, piece], ydev[d])

    def y_wait(i, piece):
        arrived(a_ref(i, y, core, 0, chunks[i][2]), y_send, y_recv.at[i, piece])

    def y_forward(i):
        n = chunks[i][2] // 2
        for d in range(2):
            ref = a_ref(i, down if d == 0 else up, core, d * n, n)
            go(ref, ref, y_send, y_recv.at[i, 2], ydev[d])

    def y_last(i):
        y_wait(i, 2)

    ys = [y, up, down, across]

    def sib_start(i, j):
        ref = a_ref(i, ys[j], core, 0, chunks[i][2])
        go(ref, ref, s_send, s_recv.at[i], sibling)

    def sib_wait(i):
        o, t0, n = chunks[i]
        arrived(abuf.at[o, pl.ds(0, 4), pl.ds(t0, n), :], s_send, s_recv.at[i])

    nb = 2 * rows

    def blocks(i):
        def pick(*of):
            return jnp.where(i == 0, of[0], jnp.where(i == 1, of[1], jnp.where(i == 2, of[2], of[3])))

        def block(along_z, along_x, second):
            bz, bx = z + along_z * (mz - z), x + along_x * (mx - x)
            return (bz + second * (pair(bz) - bz)) * 2 + bx // 2

        return [
            block(pick(0, 1, 0, 1), pick(0, 0, 1, 1), pick(0, 0, 1, 0)),
            block(pick(0, 0, 1, 1), pick(1, 0, 0, 1), pick(0, 1, 1, 1)),
        ]

    def dot(a, w):
        return lax.dot_general(a, w, (((1,), (1,)), ((), ())), preferred_element_type=F32)

    def product(o, t0, nt, ns, lo=0, hi=width):
        w = [wbuf[n // 2, pl.ds(2 * lax.rem(n, 2), 2), :, lo:hi].reshape(nb, hi - lo) for n in ns]
        a = [abuf[o, k, pl.ds(t0, nt), :] for k in range(lo // kh, hi // kh)]
        return dot(jnp.concatenate(a, axis=1), w[0] if len(w) == 1 else jnp.concatenate(w, axis=0))

    def out_start(g, n, i):
        ts = pl.ds(*groups[g])
        go(obuf.at[n, ts, :], ibuf.at[n, ts, :], o_send, o_recv.at[i], pz_dev if g == 0 else px_dev)

    def out_wait(i):
        arrived(ibuf.at[pl.ds(0, 6), pl.ds(*groups[i]), :] if i < 2 else ibuf.at[0], o_send, o_recv.at[i])

    def nbr_product(g, ns):
        v = product(1, *groups[g], ns).astype(BF16)
        for j, n in enumerate(ns):
            obuf[n, pl.ds(*groups[g]), :] = v[:, j * nb:(j + 1) * nb]
        for n in ns:
            out_start(g, n, g)

    def own_product(t0, nt, ns):
        v = product(0, t0, nt, ns)
        for j, n in enumerate(ns):
            ts = pl.ds(t0, nt)
            at = pl.ds(pl.multiple_of(n * nb, nb), nb)
            acc[n, ts, :] = v[:, j * nb:(j + 1) * nb] + resv[ts, at].astype(F32)

    def finish(n, t0, nt):
        ts = pl.ds(t0, nt)
        hid = (acc[n, ts, :] + ibuf[n, ts, :].astype(F32)).astype(BF16)
        hidden_o[ts, pl.ds(pl.multiple_of(n * nb, nb), nb)] = hid
        wide = hid.astype(F32)
        squares[ts, :] += wide * wide

    zero = r // NR

    def each(lo, hi, f):
        pl.loop(zero + lo, zero + hi)(f)

    for p in range(2):
        load_wait(wbuf.at[z, x, pl.ds(p * part, part), :], p)
        mate_start(0, p)
        if p == 0:
            nbr_start(0)
            load_wait(abuf.at[0, r], 4)
            y_start(0)
    for p in range(2):
        load_wait(wother.at[pl.ds(p * part, part), :], 2 + p)
        pair_start(1, p)
        pair_start(2, p)
    sib_start(0, 0)
    y_wait(0, 0)
    y_forward(0)
    pair_wait(1, 0)
    mate_start(1, 0)
    nbr_start(1)
    y_wait(0, 1)
    sib_start(0, 1)
    sib_start(0, 2)
    pair_wait(1, 1)
    mate_start(1, 1)
    nbr_wait(0)
    y_start(1)
    sib_start(1, 0)
    y_last(0)
    sib_start(0, 3)
    pair_wait(2, 0)
    mate_start(2, 0)
    y_wait(1, 0)
    y_forward(1)
    pair_wait(2, 1)
    pl.semaphore_signal(gate, inc=1, device_id=diag_dev, device_id_type=MESH)
    mate_start(2, 1)
    nbr_wait(1)
    y_start(2)
    sib_start(2, 0)
    y_wait(1, 1)
    sib_start(1, 1)
    sib_start(1, 2)
    pl.semaphore_wait(gate, 1)
    pair_start(3, 0)
    pair_start(3, 1)
    sib_wait(0)
    load_wait(resv, 5)
    mate_wait(0)
    each(0, 1, lambda i: own_product(0, t1, blocks(i)))
    pair_wait(3, 0)
    mate_start(3, 0)
    y_last(1)
    sib_start(1, 3)
    sib_wait(1)
    each(0, 1, lambda i: nbr_product(0, blocks(i)))
    pair_wait(3, 1)
    mate_start(3, 1)
    forward_start(0)
    forward_start(1)
    y_wait(2, 0)
    y_forward(2)
    y_start(3)
    sib_start(3, 0)
    each(1, 2, lambda i: nbr_product(0, blocks(i)))
    each(1, 2, lambda i: own_product(0, t1, blocks(i)))
    mate_wait(1)
    forward_start(2)
    y_wait(2, 1)
    sib_start(2, 1)
    sib_start(2, 2)
    mate_wait(2)
    for j in range(3, 6):
        forward_start(j)
    each(2, 3, lambda i: nbr_product(0, blocks(i)))
    y_last(2)
    sib_start(2, 3)
    sib_wait(2)
    each(0, 2, lambda i: nbr_product(1, blocks(i)))
    y_wait(3, 0)
    y_forward(3)
    y_start(4)
    sib_start(4, 0)
    each(2, 3, lambda i: nbr_product(1, blocks(i)))
    each(2, 3, lambda i: own_product(0, t1, blocks(i)))
    y_wait(3, 1)
    sib_start(3, 1)
    sib_start(3, 2)
    squares[...] = jnp.zeros_like(squares)

    out_wait(0)

    @pl.loop(0, 3)
    def _(i):
        for n in blocks(i):
            finish(n, 0, t1)

    forward_wait(0)
    first, last = blocks(3)

    @pl.loop(0, 2)
    def _(h):
        ts = pl.ds(pl.multiple_of(h * ht, ht), ht)
        obuf[first, ts, :] = product(1, ts.start, ht, [first]).astype(BF16)

    out_start(0, first, 3)
    out_start(1, first, 2)
    y_last(3)
    sib_start(3, 3)
    sib_wait(3)
    each(0, 1, lambda i: own_product(t1, t2 - t1, blocks(i)))
    y_wait(4, 0)
    y_forward(4)
    each(1, 3, lambda i: own_product(t1, t2 - t1, blocks(i)))
    forward_wait(1)

    @pl.loop(0, 2)
    def _(h):
        ts = pl.ds(pl.multiple_of(h * ht, ht), ht)
        early[ts, :] = product(1, ts.start, ht, [last], 0, late)

    y_wait(4, 1)
    sib_start(4, 1)
    sib_start(4, 2)
    forward_wait(2)

    @pl.loop(0, 2)
    def _(i):
        ts = pl.ds(pl.multiple_of((1 - i) * ht, ht), ht)
        obuf[last, ts, :] = (early[ts, :] + product(1, ts.start, ht, [last], late, width)).astype(BF16)

        @pl.when(i == 0)
        def _():
            out_start(1, last, 3)

        @pl.when(i == 1)
        def _():
            out_start(0, last, 2)

    y_last(4)
    sib_start(4, 3)
    pl.loop(0, 2)(lambda i: own_product(pl.multiple_of(i * (t2 // 2), t2 // 2), t2 // 2, [first, last]))
    sib_wait(4)
    out_wait(1)

    @pl.loop(0, 2)
    def _(i):
        own_product(t2, tokens - t2, blocks(2 * i) + blocks(2 * i + 1))
        for j in range(3):
            k = 3 * i + j
            one, other = blocks(k // 2)
            finish(jnp.where(lax.rem(k, 2) == 0, one, other), t1, t2 - t1)

    served = pltpu.make_async_copy(
        wbuf.at[:, :, :, pl.ds(pl.multiple_of((c // 2) * kh, kh), kh)], served_o, l_sem.at[6])
    served.start()

    @pl.loop(0, 3)
    def _(i):
        for n in blocks(i):
            finish(n, t2, tokens - t2)

    for i, n in ((2, first), (3, last)):
        out_wait(i)
        finish(n, 0, tokens)

    for t in range(tokens // 128):
        sums[r, t:t + 1, :] = jnp.sum(squares[t * 128:(t + 1) * 128, :].T, axis=0, keepdims=True)
    for i in (3, 4, 2, 5, 1, 6, 0):
        go(sums.at[r], sums.at[r], q_send, q_recv, peers[i])
    served.wait()
    left(wbuf.at[pl.ds(0, 3)], c_send, c_recv.at[0])
    left(wbuf.at[0, pl.ds(0, 3)], p_send, p_recv.at[0, 0])
    left(abuf.at[0, 0], n_send, n_recv.at[0])
    left(abuf.at[0, pl.ds(0, 6)], y_send, y_recv.at[0, 0])
    left(abuf.at[0], s_send, s_recv.at[0])
    left(obuf, o_send, o_recv.at[0])
    arrived(sums.at[pl.ds(0, NR - 1)], q_send, q_recv)
    total = sums[0]
    for i in range(1, NR):
        total = total + sums[i]
    total_o[...] = total
    left(sums.at[pl.ds(0, NR - 1)], q_send, q_recv)


def finish(served, hidden, total, gain, served_o, hidden_o, normed_o, normv, sem):
    tokens, kw = hidden.shape
    copies = [
        pltpu.make_async_copy(hidden, hidden_o, sem.at[0]),
        pltpu.make_async_copy(served, served_o, sem.at[1]),
    ]
    for cp in copies:
        cp.start()
    inv = lax.rsqrt(total[...] / (NR * kw) + 1e-05)
    g = gain[...].astype(F32)[None, :]
    for t in range(tokens // 128):
        ts = slice(t * 128, (t + 1) * 128)
        scale = jnp.broadcast_to(inv[t:t + 1, :], (128, 128)).T
        for i in range(kw // 128):
            ls = slice(i * 128, (i + 1) * 128)
            normv[ts, ls] = (hidden[ts, ls].astype(F32) * scale * g[:, ls]).astype(BF16)
        cp = pltpu.make_async_copy(normv.at[ts, :], normed_o.at[ts, :], sem.at[2 + t])
        cp.start()
        copies.append(cp)
    for cp in copies:
        cp.wait()


def per_device(attention_out, residual, trainer_shard, norm_gain):
    tokens, kw = attention_out.shape
    rows, width = trainer_shard.shape
    kh = kw // 2
    hbm = pl.BlockSpec(memory_space=pltpu.HBM)
    vmem = pl.BlockSpec(memory_space=pltpu.VMEM)
    dma = pltpu.SemaphoreType.DMA
    shapes = (
        jax.ShapeDtypeStruct((NX, NX, rows, kw // 2), BF16),
        jax.ShapeDtypeStruct((tokens, kw), BF16),
        jax.ShapeDtypeStruct((tokens, kw), BF16),
    )
    served, hidden, total = pl.pallas_call(
        kernel,
        out_shape=tuple(pltpu.VMEM(a.shape, a.dtype) for a in shapes[:2]) + (pltpu.VMEM((tokens // 128, 128), F32),),
        in_specs=[hbm] * 3,
        out_specs=(vmem,) * 3,
        scratch_shapes=[
            pltpu.VMEM((NX, NX, rows, NR * kh), BF16),
            pltpu.VMEM((rows, NR * kh), BF16),
            pltpu.VMEM((2, NR, tokens, kh), BF16),
            pltpu.VMEM((NR, tokens, 2 * rows), F32),
            pltpu.VMEM((NR, tokens, 2 * rows), BF16),
            pltpu.VMEM((NR, tokens, 2 * rows), BF16),
            pltpu.VMEM((tokens, kw), BF16),
            pltpu.VMEM((tokens, 2 * rows), F32),
            pltpu.VMEM((tokens, 128), F32),
            pltpu.VMEM((NR, tokens // 128, 128), F32),
            dma(()), dma((6,)),
            dma(()), dma((3, 2)),
            dma(()), dma((2,)),
            dma(()), dma((5, 3)),
            dma(()), dma((5,)),
            dma(()), dma((4,)),
            dma(()), dma(()),
            dma((7,)),
            pltpu.SemaphoreType.REGULAR,
        ],
        compiler_params=pltpu.CompilerParams(
            collective_id=0, has_side_effects=True, vmem_limit_bytes=50 * 1024 * 1024
        ),
        cost_estimate=pl.CostEstimate(
            flops=2 * tokens * kw * width, bytes_accessed=10 * tokens * kw, transcendentals=0
        ),
    )(attention_out, residual, trainer_shard)
    served, hidden, normed = pl.pallas_call(
        finish,
        out_shape=shapes,
        in_specs=[vmem] * 4,
        out_specs=(hbm,) * 3,
        scratch_shapes=[pltpu.VMEM((tokens, kw), BF16), dma((2 + tokens // 128,))],
        compiler_params=pltpu.CompilerParams(vmem_limit_bytes=16 * 1024 * 1024),
        cost_estimate=pl.CostEstimate(
            flops=4 * tokens * kw, bytes_accessed=5 * tokens * kw, transcendentals=tokens
        ),
    )(served, hidden, total, norm_gain)
    return (served.reshape(NX * NX * rows, kw // 2), hidden, normed)


def solution(mesh):
    in_specs = (P("col", "row"), P("col", "row"), P(("row", "col"), None), P("row"))
    out_specs = (P("row", "col"), P("col", "row"), P("col", "row"))
    return jax.shard_map(
        per_device, mesh=mesh, in_specs=in_specs, out_specs=out_specs, check_vma=False
    )
```
